32 devices in a mesh: groups: 2 (over x), blk: 4 (over y, core), dp: 4 (over z).
Axes of the slice: x: 2, y: 2, z: 4, core: 2. Of those that a mesh axis runs over, the one named last changes fastest.
Arguments:
- data: bfloat16 [30720, 768], P(('groups', 'blk', 'dp')), parts along dimension 0, may hold values from -6 to 6
- landmarks: bfloat16 [8192, 768], P(('groups', 'blk')), parts along dimension 0, may hold values from -6 to 6
- basis: bfloat16 [8192, 512], P(('groups', 'blk')), parts along dimension 0, may hold values from -6 to 6
Outputs:
- new_basis: float32 [8192, 512], P(('groups', 'blk')), parts along dimension 0
The draws below stay inside these ranges and needn't reach their ends.
There are 2 independent parts, one for each index of `groups`. The reference program is written for one: setup_inputs(seed, part) draws one part's arguments, and reference() takes and returns one part's arrays. A program takes and returns all parts, laid end to end along the dimension named above; each array names one. Nothing has to cross between parts.
All inputs are finite; a program needn't handle non-finite values.
Results may differ from the reference program's by a relative error of at most 0.0057.
The reference program's roundings to bfloat16 on the way count: a program that leaves them out, or rounds other values in their place, can miss the bound.
Values may be sent and summed in bfloat16 or wider, within the bound.
No kernel may reach another device: no remote copies, remote signals or barrier semaphores. Data moves between devices by JAX's collectives and lax.ppermute only.
A program may use at most 128 MiB of HBM per device.

```python
import math
import jax
import jax.numpy as jnp
from jax import lax

D = 768
LANDMARKS = 4096
K = 512
ROWS = 15360


def steps_of(rng, shape, split, least, top_value):
    loudness = 1.0
    for position, shards_of in split:
        steps = jax.random.uniform(jax.random.fold_in(jax.random.fold_in(rng, 6), position), (shards_of,), jnp.float32, least / len(split), top_value / len(split))
        loudness = loudness * jnp.repeat(jnp.exp(steps), shape[position] // shards_of).reshape((-1,) + (1,) * (len(shape) - 1 - position))
    return loudness


def noise(key, extent, scale, bound, shards=(), dtype=jnp.bfloat16):
    drawn = jax.random.normal(key, extent, jnp.float32) * scale
    if len(shards) > 0:
        drawn = steps_of(key, extent, shards, -0.22, 0.18) * drawn
    return jnp.clip(drawn, min=-bound, max=bound).astype(dtype)


def setup_inputs(seed: int = 0, part: int = 0) -> dict:
    splits = jax.random.split(jax.random.key(seed), 4)
    part_splits = jax.random.split(jax.random.fold_in(splits[3], part), 4)
    return {
        "data": noise(part_splits[0], (ROWS, D), 1.0, 6.0, ((0, 16),)),
        "landmarks": noise(part_splits[1], (LANDMARKS, D), 1.0, 6.0, ((0, 4),)),
        "basis": noise(part_splits[2], (LANDMARKS, K), 1.0, 6.0, ((0, 4),)),
    }


NORM_EPS = 1e-06

def unit_rows(values):
    wide = values.astype(jnp.float32)
    return (wide * lax.rsqrt(lax.optimization_barrier(jnp.sum(wide * wide, axis=1, keepdims=True)) + NORM_EPS)).astype(jnp.bfloat16)

def kernel_tile(unit_data, unit_marks):
    scores = lax.dot_general(unit_data.astype(jnp.float32), unit_marks.astype(jnp.float32), (((1,), (1,)), ((), ())), preferred_element_type=jnp.float32)
    return jnp.exp(math.sqrt(D) * scores).astype(jnp.bfloat16)

def reference(data, landmarks, basis):
    unit_data = unit_rows(data)
    unit_marks = unit_rows(landmarks)
    row_block = math.gcd(ROWS, 2048)
    blocks = unit_data.reshape(ROWS // row_block, row_block, D)

    def forward(rows_here):
        return jnp.dot(kernel_tile(rows_here, unit_marks).astype(jnp.float32), basis.astype(jnp.float32), preferred_element_type=jnp.float32)
    projected = lax.map(forward, blocks).reshape(ROWS, K)
    column_mean = lax.optimization_barrier(jnp.mean(projected, axis=0))
    centred = (projected - column_mean).astype(jnp.bfloat16).reshape(ROWS // row_block, row_block, K)

    def backward(running, pair):
        rows_here, centred_here = pair
        tile = kernel_tile(rows_here, unit_marks)
        return (running + lax.dot_general(tile.astype(jnp.float32), centred_here.astype(jnp.float32), (((0,), (0,)), ((), ())), preferred_element_type=jnp.float32), None)
    back, _ = lax.scan(backward, jnp.zeros((LANDMARKS, K), jnp.float32), (blocks, centred))
    gram = lax.dot_general(back, back, (((0,), (0,)), ((), ())), precision=lax.Precision.HIGHEST)
    lower_factor = jnp.linalg.cholesky(gram)
    solved = lax.linalg.triangular_solve(lower_factor, back, left_side=False, lower=True, transpose_a=True)
    return solved * math.sqrt(LANDMARKS)
```

```python
import functools
import math

import jax
import jax.numpy as jnp
from jax import lax
from jax.experimental import pallas as pl
from jax.experimental.pallas import tpu as pltpu
from jax.sharding import PartitionSpec as P

NORM_EPS = 1e-06
BLOCK = 128
PANEL = 8
HIGHEST = lax.Precision.HIGHEST
SWAP_CORE = [(0, 1), (1, 0), (2, 3), (3, 2)]
SWAP_Y = [(0, 2), (2, 0), (1, 3), (3, 1)]
SWAP_INNER = [(1, 2), (2, 1)]
TO_INNER = [(0, 1), (3, 2)]
TO_OUTER = [(1, 0), (2, 3)]
SWAP_NEAR = [(0, 1), (1, 0), (2, 3), (3, 2)]
SWAP_FAR = [(0, 2), (2, 0), (1, 3), (3, 1)]


def unit_rows(values):
    wide = values.astype(jnp.float32)
    return (wide * lax.rsqrt(jnp.sum(wide * wide, axis=1, keepdims=True) + NORM_EPS)).astype(
        jnp.bfloat16
    )


def kernel_tile(unit_data, unit_marks, exponent_scale):
    scores = lax.dot_general(
        unit_data, unit_marks, (((1,), (1,)), ((), ())), preferred_element_type=jnp.float32
    )
    return jnp.exp(exponent_scale * scores).astype(jnp.bfloat16)


def spread_row(tile, row):
    return jnp.broadcast_to(tile[row : row + 1, :], tile.shape)


def lower_inverse(square):
    size = square.shape[0]
    groups = size // PANEL
    lane = lax.broadcasted_iota(jnp.int32, (PANEL, size), 1)
    rows = [square[PANEL * g : PANEL * (g + 1), :] for g in range(groups)]
    finished = []
    for p in range(groups):
        live = range(groups - p)
        columns = [
            [
                jnp.broadcast_to(
                    rows[p + g][:, PANEL * p + k : PANEL * p + k + 1], (PANEL, size)
                )
                for g in live
            ]
            for k in range(PANEL)
        ]
        for k in range(PANEL):
            position = PANEL * p + k
            pivot = spread_row(columns[k][0], k)
            inverse = 1.0 / pivot
            row = jnp.where(lane == position, 1.0, spread_row(rows[p], k))
            finished.append((jnp.where(lane <= position, row, 0.0) * lax.rsqrt(pivot))[:1])
            scaled = row * inverse
            for m in range(k + 1, PANEL):
                ratio = spread_row(columns[k][0], m) * inverse
                for g in live:
                    columns[m][g] = columns[m][g] - columns[k][g] * ratio
            for g in live:
                rows[p + g] = (
                    jnp.where(lane == position, 0.0, rows[p + g]) - columns[k][g] * scaled
                )
    return jnp.concatenate(finished, 0)


def times_transposed(left, right):
    return lax.dot_general(
        left,
        right,
        (((1,), (1,)), ((), ())),
        precision=HIGHEST,
        preferred_element_type=jnp.float32,
    )


def eliminate(scale, left_ref, rows_ref, inverse_ref, write):
    order = left_ref.shape[0]
    blocks = order // BLOCK

    def step(position, carry):
        here = pl.ds(pl.multiple_of(position * BLOCK, BLOCK), BLOCK)
        inverse_ref[...] = lower_inverse(left_ref[here, here])
        for b in range(blocks):

            @pl.when(position == b)
            def _():
                now = slice(b * BLOCK, (b + 1) * BLOCK)
                later = slice((b + 1) * BLOCK, order)
                inverse = inverse_ref[...]
                solved = times_transposed(rows_ref[:, now], inverse)
                if b + 1 < blocks:
                    factor = times_transposed(left_ref[later, now], inverse)
                    left_ref[later, later] -= times_transposed(factor, factor)
                    rows_ref[:, later] -= times_transposed(solved, factor)
                write(now, solved * scale)

        return carry

    lax.fori_loop(0, blocks, step, 0)


def whiten_kernel(scale, gram_ref, rows_ref, out_ref, left_ref, moved_ref, inverse_ref):
    left_ref[...] = gram_ref[...]
    moved_ref[...] = rows_ref[...]

    def write(now, values):
        out_ref[:, now] = values

    eliminate(scale, left_ref, moved_ref, inverse_ref, write)


def first_kernel(gram_ref, rows_ref, out_ref, back_ref, left_ref, moved_ref, inverse_ref):
    count, order = rows_ref.shape
    left_ref[...] = gram_ref[...]
    moved_ref[:count, :] = rows_ref[...]
    shape = (order, order)
    moved_ref[count:, :] = jnp.where(
        lax.broadcasted_iota(jnp.int32, shape, 0) == lax.broadcasted_iota(jnp.int32, shape, 1),
        1.0,
        0.0,
    )

    def write(now, values):
        out_ref[:, now] = values[:count]
        back_ref[:, now] = values[count:]

    eliminate(1.0, left_ref, moved_ref, inverse_ref, write)


def second_kernel(
    scale, gram_ref, rows_ref, done_ref, solve_ref, out_ref, left_ref, moved_ref, inverse_ref
):
    order = rows_ref.shape[1]
    factor = lax.dot_general(
        gram_ref[:, :order],
        solve_ref[...],
        (((1,), (0,)), ((), ())),
        precision=HIGHEST,
        preferred_element_type=jnp.float32,
    )
    left_ref[...] = gram_ref[:, order:] - times_transposed(factor, factor)
    moved_ref[...] = rows_ref[...] - times_transposed(done_ref[...], factor)
    out_ref[:, :order] = done_ref[...] * scale

    def write(now, values):
        out_ref[:, order + now.start : order + now.stop] = values

    eliminate(scale, left_ref, moved_ref, inverse_ref, write)


def solve_call(kernel, out_shapes, moved_shape, *operands):
    vmem = pl.BlockSpec(memory_space=pltpu.VMEM)
    single = len(out_shapes) == 1
    shapes = [jax.ShapeDtypeStruct(shape, jnp.float32) for shape in out_shapes]
    order = moved_shape[1]
    return pl.pallas_call(
        kernel,
        out_shape=shapes[0] if single else shapes,
        in_specs=[vmem] * len(operands),
        out_specs=vmem if single else [vmem] * len(shapes),
        scratch_shapes=[
            pltpu.VMEM((order, order), jnp.float32),
            pltpu.VMEM(moved_shape, jnp.float32),
            pltpu.VMEM((BLOCK, BLOCK), jnp.float32),
        ],
        compiler_params=pltpu.CompilerParams(vmem_limit_bytes=32 * 2**20),
    )(*operands)


def whiten(gram_matrix, rows, scale):
    kernel = functools.partial(whiten_kernel, scale)
    return solve_call(kernel, [rows.shape], rows.shape, gram_matrix, rows)


def whiten_first(gram_matrix, rows):
    count, order = rows.shape
    return solve_call(
        first_kernel, [rows.shape, (order, order)], (count + order, order), gram_matrix, rows
    )


def whiten_second(gram_rows, rows, done, solve, scale):
    count, order = rows.shape
    kernel = functools.partial(second_kernel, scale)
    return solve_call(
        kernel, [(count, 2 * order)], rows.shape, gram_rows, rows, done, solve
    )


def own_gram(rows):
    return lax.dot_general(rows, rows, (((0,), (0,)), ((), ())), precision=HIGHEST)


def general_body(data, landmarks, basis):
    exponent_scale = math.sqrt(data.shape[1])
    all_marks = landmarks.shape[0] * lax.axis_size("blk")
    total_rows = data.shape[0] * lax.axis_size("blk") * lax.axis_size("dp")
    tile = kernel_tile(
        unit_rows(data),
        lax.all_gather(unit_rows(landmarks), "blk", axis=0, tiled=True),
        exponent_scale,
    )
    projected = jnp.dot(
        tile, lax.all_gather(basis, "blk", axis=0, tiled=True), preferred_element_type=jnp.float32
    )
    column_sums = lax.psum(lax.psum(jnp.sum(projected, axis=0), "blk"), "dp")
    centred = (projected - column_sums / total_rows).astype(jnp.bfloat16)
    partial = lax.dot_general(
        tile, centred, (((0,), (0,)), ((), ())), preferred_element_type=jnp.float32
    )
    panel = lax.psum_scatter(partial, "blk", scatter_dimension=0, tiled=True)
    shares = lax.psum_scatter(panel, "dp", scatter_dimension=0, tiled=True)
    gram_matrix = lax.psum(own_gram(shares), ("blk", "dp"))
    local_rows = whiten(gram_matrix, shares, math.sqrt(all_marks))
    return lax.all_gather(local_rows, "dp", axis=0, tiled=True)


def over_cores(values):
    return lax.ppermute(values, "blk", SWAP_CORE)


def over_y(values):
    return lax.ppermute(values, "blk", SWAP_Y)


def after(values, *others):
    return lax.optimization_barrier((values, *others))[0]


def product_of(left, right):
    return lax.dot_general(left, right, (((0,), (0,)), ((), ())), precision=HIGHEST)


def product(left, right):
    return jnp.dot(left, right, preferred_element_type=jnp.float32)


def column_stats(tile):
    wide = tile.astype(jnp.float32)
    return jnp.concatenate(
        [jnp.sum(wide, axis=0, keepdims=True), jnp.max(wide, axis=0, keepdims=True)], 0
    )


def joined(stats, other):
    return jnp.concatenate([stats[:1] + other[:1], jnp.maximum(stats[1:], other[1:])], 0)


def weighted_rows(weights, rows):
    top = lax.reduce_precision(weights, 8, 7)
    middle = lax.reduce_precision(weights - top, 8, 7)
    parts = jnp.concatenate([top, middle, weights - top - middle], 0).astype(jnp.bfloat16)
    value = jnp.sum(product(parts, rows), axis=0, keepdims=True)
    size = product(top.astype(jnp.bfloat16), jnp.abs(rows))
    return jnp.concatenate([value, size], 0)


def as_half(values):
    return lax.optimization_barrier(values.astype(jnp.float16))


def body(data, landmarks, basis):
    exponent_scale = math.sqrt(data.shape[1])
    row_count = data.shape[0]
    all_marks = landmarks.shape[0] * lax.axis_size("blk")
    total_rows = row_count * lax.axis_size("blk") * lax.axis_size("dp")
    second = lax.axis_index("blk") % 2 == 1
    place = lax.axis_index("dp")
    odd = place % 2 == 1
    inner = (place == 1) | (place == 2)
    half_marks = landmarks.shape[0] // 2
    width = basis.shape[1] // 2

    def own_half(values):
        middle = values.shape[1] // 2
        return jnp.where(odd, values[:, middle:], values[:, :middle])

    def whole(half, other):
        return jnp.concatenate([jnp.where(odd, other, half), jnp.where(odd, half, other)], 1)

    def over_near(values):
        return lax.ppermute(values, "dp", SWAP_NEAR)

    def tile_of(marks):
        return kernel_tile(unit_data, unit_rows(marks), exponent_scale)

    mark_halves = [over_y(own_half(landmarks[:half_marks])), over_y(own_half(landmarks[half_marks:]))]
    unit_data = unit_rows(jnp.concatenate([data, over_cores(data)], 0))
    near_tiles = [tile_of(landmarks[:half_marks]), tile_of(landmarks[half_marks:])]
    basis_parts = [basis[:, :width], basis[:, width:]]
    near_parts = [
        product(near_tiles[0], part[:half_marks]) + product(near_tiles[1], part[half_marks:])
        for part in basis_parts
    ]
    mark_halves[0] = after(mark_halves[0], *near_tiles)
    other_first = over_near(mark_halves[0])
    basis_halves = [over_y(after(own_half(basis_parts[0]), mark_halves[0]))]
    mark_halves[1] = after(mark_halves[1], *near_parts)
    other_second = over_near(mark_halves[1])
    basis_halves.append(over_y(after(own_half(basis_parts[1]), mark_halves[1])))
    far_tiles = [tile_of(whole(mark_halves[0], other_first))]
    basis_halves[0] = after(basis_halves[0], far_tiles[0])
    basis_others = [over_near(basis_halves[0])]
    far_tiles.append(tile_of(whole(mark_halves[1], other_second)))
    near_stats = jnp.concatenate([column_stats(tile) for tile in near_tiles], 1)
    far_stats = jnp.concatenate([column_stats(tile) for tile in far_tiles], 1)
    stats = jnp.concatenate([near_stats, far_stats], 1)
    stats = joined(stats, over_y(jnp.concatenate([far_stats, near_stats], 1)))
    basis_others.append(over_near(basis_halves[1]))
    stats = joined(stats, over_near(stats))
    stats = joined(stats, lax.ppermute(stats, "dp", SWAP_FAR))
    sums = [stats[:1, : 2 * half_marks], stats[:1, 2 * half_marks :]]
    peaks = stats[1:].reshape(4, half_marks, 1)

    def centred_of(near_basis, near_part, half, other):
        far_basis = whole(half, other)
        part = (
            near_part
            + product(far_tiles[0], far_basis[:half_marks])
            + product(far_tiles[1], far_basis[half_marks:])
        )
        projected = part[:row_count] + over_cores(part[row_count:])
        weighed = weighted_rows(sums[0], near_basis) + weighted_rows(sums[1], far_basis)
        weighed = weighed + over_cores(weighed)
        centred = (projected - weighed[:1] / total_rows).astype(jnp.bfloat16)
        scale = 2.0**14 / (1.02 * jnp.maximum(weighed[1:], 1e-30))
        return jnp.concatenate([centred, over_cores(centred)], 0), scale

    def back_of(index, centred, scale):
        def part_of(tile, peak):
            part = lax.dot_general(
                tile, centred, (((0,), (0,)), ((), ())), preferred_element_type=jnp.float32
            )
            return part * (scale * (1.0 / peak))

        sent = over_y(as_half(part_of(far_tiles[index], peaks[2 + index])))
        panel = part_of(near_tiles[index], peaks[index]) + sent.astype(jnp.float32)
        outer = lax.ppermute(as_half(panel), "dp", TO_INNER)
        pair = as_half(panel + outer.astype(jnp.float32))
        crossed = lax.ppermute(pair, "dp", SWAP_INNER)
        total = as_half(pair.astype(jnp.float32) + crossed.astype(jnp.float32))
        given = lax.ppermute(total, "dp", TO_OUTER)
        total = jnp.where(inner, total, given).astype(jnp.float32)
        return total * (peaks[index] * 2.0**-14)

    def summed(part):
        middle = part.shape[0] // 2
        top, bottom = part[:middle], part[middle:]
        kept = jnp.where(second, bottom, top) + over_cores(jnp.where(second, top, bottom))
        kept = kept + over_y(kept)
        others = over_cores(kept)
        return jnp.concatenate(
            [jnp.where(second, others, kept), jnp.where(second, kept, others)], 0
        )

    centred = [
        centred_of(*parts) for parts in zip(basis_parts, near_parts, basis_halves, basis_others)
    ]
    first, last = [
        jnp.concatenate([back_of(0, *pair), back_of(1, *pair)], 0) for pair in centred
    ]
    first_gram = summed(product_of(first, first))
    last_gram = summed(jnp.concatenate([product_of(last, first), product_of(last, last)], 1))
    done, solve = whiten_first(first_gram, first)
    return whiten_second(last_gram, last, done, solve, math.sqrt(all_marks))


def solution(mesh):
    in_specs = (
        P(("groups", "blk", "dp"), None),
        P(("groups", "blk"), None),
        P(("groups", "blk"), None),
    )
    out_specs = P(("groups", "blk"), None)
    fits = mesh.shape["blk"] == 4 and mesh.shape["dp"] == 4
    return jax.shard_map(
        body if fits else general_body,
        mesh=mesh,
        in_specs=in_specs,
        out_specs=out_specs,
        check_vma=False,
    )
```

```python
import functools
import math

import jax
import jax.numpy as jnp
from jax import lax
from jax.experimental import pallas as pl
from jax.experimental.pallas import tpu as pltpu
from jax.sharding import PartitionSpec as P

NORM_EPS = 1e-06
BLOCK = 128
PANEL = 8
HIGHEST = lax.Precision.HIGHEST
SWAP_CORE = [(0, 1), (1, 0), (2, 3), (3, 2)]
SWAP_Y = [(0, 2), (2, 0), (1, 3), (3, 1)]
SWAP_INNER = [(1, 2), (2, 1)]
TO_INNER = [(0, 1), (3, 2)]
TO_OUTER = [(1, 0), (2, 3)]
SWAP_NEAR = [(0, 1), (1, 0), (2, 3), (3, 2)]
ACROSS = [(0, 3), (3, 0), (1, 2), (2, 1)]
SWAP_FAR = [(0, 2), (2, 0), (1, 3), (3, 1)]


def unit_rows(values):
    wide = values.astype(jnp.float32)
    return (wide * lax.rsqrt(jnp.sum(wide * wide, axis=1, keepdims=True) + NORM_EPS)).astype(
        jnp.bfloat16
    )


def kernel_tile(unit_data, unit_marks, exponent_scale):
    scores = lax.dot_general(
        unit_data, unit_marks, (((1,), (1,)), ((), ())), preferred_element_type=jnp.float32
    )
    return jnp.exp(exponent_scale * scores).astype(jnp.bfloat16)


def spread_row(tile, row):
    return jnp.broadcast_to(tile[row : row + 1, :], tile.shape)


def lower_inverse(square):
    size = square.shape[0]
    groups = size // PANEL
    lane = lax.broadcasted_iota(jnp.int32, (PANEL, size), 1)
    rows = [square[PANEL * g : PANEL * (g + 1), :] for g in range(groups)]
    finished = []
    for p in range(groups):
        live = range(groups - p)
        columns = [
            [
                jnp.broadcast_to(
                    rows[p + g][:, PANEL * p + k : PANEL * p + k + 1], (PANEL, size)
                )
                for g in live
            ]
            for k in range(PANEL)
        ]
        for k in range(PANEL):
            position = PANEL * p + k
            pivot = spread_row(columns[k][0], k)
            inverse = 1.0 / pivot
            row = jnp.where(lane == position, 1.0, spread_row(rows[p], k))
            finished.append((jnp.where(lane <= position, row, 0.0) * lax.rsqrt(pivot))[:1])
            scaled = row * inverse
            for m in range(k + 1, PANEL):
                ratio = spread_row(columns[k][0], m) * inverse
                for g in live:
                    columns[m][g] = columns[m][g] - columns[k][g] * ratio
            for g in live:
                rows[p + g] = (
                    jnp.where(lane == position, 0.0, rows[p + g]) - columns[k][g] * scaled
                )
    return jnp.concatenate(finished, 0)


def times_transposed(left, right):
    return lax.dot_general(
        left,
        right,
        (((1,), (1,)), ((), ())),
        precision=HIGHEST,
        preferred_element_type=jnp.float32,
    )


def eliminate(scale, left_ref, rows_ref, inverse_ref, write):
    order = left_ref.shape[0]
    blocks = order // BLOCK

    def step(position, carry):
        here = pl.ds(pl.multiple_of(position * BLOCK, BLOCK), BLOCK)
        inverse_ref[...] = lower_inverse(left_ref[here, here])
        for b in range(blocks):

            @pl.when(position == b)
            def _():
                now = slice(b * BLOCK, (b + 1) * BLOCK)
                later = slice((b + 1) * BLOCK, order)
                inverse = inverse_ref[...]
                solved = times_transposed(rows_ref[:, now], inverse)
                if b + 1 < blocks:
                    factor = times_transposed(left_ref[later, now], inverse)
                    left_ref[later, later] -= times_transposed(factor, factor)
                    rows_ref[:, later] -= times_transposed(solved, factor)
                write(now, solved * scale)

        return carry

    lax.fori_loop(0, blocks, step, 0)


def whiten_kernel(scale, gram_ref, rows_ref, out_ref, left_ref, moved_ref, inverse_ref):
    left_ref[...] = gram_ref[...]
    moved_ref[...] = rows_ref[...]

    def write(now, values):
        out_ref[:, now] = values

    eliminate(scale, left_ref, moved_ref, inverse_ref, write)


def first_kernel(gram_ref, rows_ref, out_ref, back_ref, left_ref, moved_ref, inverse_ref):
    count, order = rows_ref.shape
    left_ref[...] = gram_ref[...]
    moved_ref[:count, :] = rows_ref[...]
    shape = (order, order)
    moved_ref[count:, :] = jnp.where(
        lax.broadcasted_iota(jnp.int32, shape, 0) == lax.broadcasted_iota(jnp.int32, shape, 1),
        1.0,
        0.0,
    )

    def write(now, values):
        out_ref[:, now] = values[:count]
        back_ref[:, now] = values[count:]

    eliminate(1.0, left_ref, moved_ref, inverse_ref, write)


def second_kernel(
    scale, gram_ref, rows_ref, done_ref, solve_ref, out_ref, left_ref, moved_ref, inverse_ref
):
    order = rows_ref.shape[1]
    factor = lax.dot_general(
        gram_ref[:, :order],
        solve_ref[...],
        (((1,), (0,)), ((), ())),
        precision=HIGHEST,
        preferred_element_type=jnp.float32,
    )
    left_ref[...] = gram_ref[:, order:] - times_transposed(factor, factor)
    moved_ref[...] = rows_ref[...] - times_transposed(done_ref[...], factor)
    out_ref[:, :order] = done_ref[...] * scale

    def write(now, values):
        out_ref[:, order + now.start : order + now.stop] = values

    eliminate(scale, left_ref, moved_ref, inverse_ref, write)


def solve_call(kernel, out_shapes, moved_shape, *operands):
    vmem = pl.BlockSpec(memory_space=pltpu.VMEM)
    single = len(out_shapes) == 1
    shapes = [jax.ShapeDtypeStruct(shape, jnp.float32) for shape in out_shapes]
    order = moved_shape[1]
    return pl.pallas_call(
        kernel,
        out_shape=shapes[0] if single else shapes,
        in_specs=[vmem] * len(operands),
        out_specs=vmem if single else [vmem] * len(shapes),
        scratch_shapes=[
            pltpu.VMEM((order, order), jnp.float32),
            pltpu.VMEM(moved_shape, jnp.float32),
            pltpu.VMEM((BLOCK, BLOCK), jnp.float32),
        ],
        compiler_params=pltpu.CompilerParams(vmem_limit_bytes=32 * 2**20),
        cost_estimate=pl.CostEstimate(
            flops=160 * moved_shape[0] * order * order,
            bytes_accessed=4 * moved_shape[0] * order,
            transcendentals=0,
        ),
    )(*operands)


def whiten(gram_matrix, rows, scale):
    kernel = functools.partial(whiten_kernel, scale)
    return solve_call(kernel, [rows.shape], rows.shape, gram_matrix, rows)


def whiten_first(gram_matrix, rows):
    count, order = rows.shape
    return solve_call(
        first_kernel, [rows.shape, (order, order)], (count + order, order), gram_matrix, rows
    )


def whiten_second(gram_rows, rows, done, solve, scale):
    count, order = rows.shape
    kernel = functools.partial(second_kernel, scale)
    return solve_call(
        kernel, [(count, 2 * order)], rows.shape, gram_rows, rows, done, solve
    )


def own_gram(rows):
    return lax.dot_general(rows, rows, (((0,), (0,)), ((), ())), precision=HIGHEST)


def general_body(data, landmarks, basis):
    exponent_scale = math.sqrt(data.shape[1])
    all_marks = landmarks.shape[0] * lax.axis_size("blk")
    total_rows = data.shape[0] * lax.axis_size("blk") * lax.axis_size("dp")
    tile = kernel_tile(
        unit_rows(data),
        lax.all_gather(unit_rows(landmarks), "blk", axis=0, tiled=True),
        exponent_scale,
    )
    projected = jnp.dot(
        tile, lax.all_gather(basis, "blk", axis=0, tiled=True), preferred_element_type=jnp.float32
    )
    column_sums = lax.psum(lax.psum(jnp.sum(projected, axis=0), "blk"), "dp")
    centred = (projected - column_sums / total_rows).astype(jnp.bfloat16)
    partial = lax.dot_general(
        tile, centred, (((0,), (0,)), ((), ())), preferred_element_type=jnp.float32
    )
    panel = lax.psum_scatter(partial, "blk", scatter_dimension=0, tiled=True)
    shares = lax.psum_scatter(panel, "dp", scatter_dimension=0, tiled=True)
    gram_matrix = lax.psum(own_gram(shares), ("blk", "dp"))
    local_rows = whiten(gram_matrix, shares, math.sqrt(all_marks))
    return lax.all_gather(local_rows, "dp", axis=0, tiled=True)


def tile_kernel(exponent_scale, split, data_ref, odd_ref, *refs):
    half_refs, other_refs = refs[:split], refs[split:-3]
    tile_ref, stats_ref, unit_ref = refs[-3:]
    at = 0
    if other_refs:
        odd = odd_ref[0] == 1
        for half_ref, other_ref in zip(half_refs, other_refs):
            count, width = half_ref.shape
            here = slice(at, at + count)
            for low in (True, False):
                span = slice(0, width) if low else slice(width, 2 * width)

                @pl.when(odd == low)
                def _():
                    unit_ref[here, span] = other_ref[...]

                @pl.when(odd != low)
                def _():
                    unit_ref[here, span] = half_ref[...]

            at += count
        unit_ref[...] = unit_rows(unit_ref[...])
    else:
        unit_ref[...] = unit_rows(half_refs[0][...])
    rows = data_ref.shape[0]
    step = math.gcd(rows, 480)
    total = peak = None
    for start in range(0, rows, step):
        scores = lax.dot_general(
            data_ref[start : start + step, :],
            unit_ref[...],
            (((1,), (1,)), ((), ())),
            preferred_element_type=jnp.float32,
        )
        tile = jnp.exp(exponent_scale * scores).astype(jnp.bfloat16)
        tile_ref[start : start + step, :] = tile
        wide = tile.astype(jnp.float32)
        sums = jnp.sum(wide, axis=0, keepdims=True)
        peaks = jnp.max(wide, axis=0, keepdims=True)
        total = sums if total is None else total + sums
        peak = peaks if peak is None else jnp.maximum(peak, peaks)
    stats_ref[...] = jnp.concatenate([total, peak], 0)


def tile_call(unit_data, odd, halves, others, exponent_scale):
    vmem = pl.BlockSpec(memory_space=pltpu.VMEM)
    rows, depth = unit_data.shape
    count = sum(half.shape[0] for half in halves)
    return pl.pallas_call(
        functools.partial(tile_kernel, exponent_scale, len(halves)),
        out_shape=[
            jax.ShapeDtypeStruct((rows, count), jnp.bfloat16),
            jax.ShapeDtypeStruct((2, count), jnp.float32),
        ],
        in_specs=[vmem, pl.BlockSpec(memory_space=pltpu.SMEM)] + [vmem] * (len(halves) + len(others)),
        out_specs=[vmem, vmem],
        scratch_shapes=[pltpu.VMEM((count, depth), jnp.bfloat16)],
        compiler_params=pltpu.CompilerParams(vmem_limit_bytes=32 * 2**20),
        cost_estimate=pl.CostEstimate(
            flops=2 * rows * count * depth,
            bytes_accessed=2 * rows * (count + depth),
            transcendentals=rows * count,
        ),
    )(unit_data, odd, *halves, *others)


def over_cores(values):
    return lax.ppermute(values, "blk", SWAP_CORE)


def over_y(values):
    return lax.ppermute(values, "blk", SWAP_Y)


def after(values, *others):
    return lax.optimization_barrier((values, *others))[0]


def product_of(left, right):
    return lax.dot_general(left, right, (((0,), (0,)), ((), ())), precision=HIGHEST)


def product(left, right):
    return jnp.dot(left, right, preferred_element_type=jnp.float32)


def joined(stats, other):
    return jnp.concatenate([stats[:1] + other[:1], jnp.maximum(stats[1:], other[1:])], 0)


def weighted_rows(weights, rows):
    top = lax.reduce_precision(weights, 8, 7)
    middle = lax.reduce_precision(weights - top, 8, 7)
    parts = jnp.concatenate([top, middle, weights - top - middle], 0).astype(jnp.bfloat16)
    value = jnp.sum(product(parts, rows), axis=0, keepdims=True)
    size = product(top.astype(jnp.bfloat16), jnp.abs(rows))
    return jnp.concatenate([value, size], 0)


def as_half(values):
    return lax.optimization_barrier(values.astype(jnp.float16))


def body(data, landmarks, basis):
    exponent_scale = math.sqrt(data.shape[1])
    all_marks = landmarks.shape[0] * lax.axis_size("blk")
    total_rows = data.shape[0] * lax.axis_size("blk") * lax.axis_size("dp")
    second = lax.axis_index("blk") % 2 == 1
    place = lax.axis_index("dp")
    odd = place % 2 == 1
    inner = (place == 1) | (place == 2)
    marks = landmarks.shape[0]
    half_marks = marks // 2
    width = basis.shape[1] // 2
    pieces = 4
    piece = marks // pieces

    previous = []

    def ordered(step, operand, *others):
        if previous:
            operand = lax.optimization_barrier((operand, previous.pop()))[0]
        value = step(operand, *others)
        previous.append(jax.tree.leaves(value)[0])
        return value

    def own_half(values):
        middle = values.shape[1] // 2
        return jnp.where(odd, values[:, middle:], values[:, :middle])

    def over_near(values):
        return lax.ppermute(values, "dp", SWAP_NEAR)

    def far_product(tile, rows, part):
        return part + product(tile, rows)

    basis_parts = [basis[:, :width], basis[:, width:]]
    near_marks = [landmarks[:half_marks], landmarks[half_marks:]]
    received = [
        over_y(own_half(landmarks[start : start + piece])) for start in range(0, marks, piece)
    ]
    unit_data = unit_rows(jnp.concatenate([data, over_cores(data)], 0))
    parity = (place % 2).astype(jnp.int32).reshape(1)
    tiles, tile_stats = [], []

    def add_tile(halves, others=()):
        tile, stats = ordered(
            lambda first: tile_call(unit_data, parity, [first, *halves[1:]], others, exponent_scale),
            halves[0],
        )
        tiles.append(tile)
        tile_stats.append(stats)

    def arrived(values):
        return ordered(lambda value: value, values)

    def mark_arrived(index):
        mark_halves.append(arrived(received[index]))
        mark_others.append(over_near(mark_halves[index]))

    mark_halves, mark_others = [], []
    add_tile(near_marks[:1])
    far_basis = [over_y(after(basis_parts[0], tiles[0]))]
    mark_arrived(0)
    add_tile(near_marks[1:])
    far_basis.append(over_y(after(basis_parts[1], tiles[1])))
    mark_arrived(1)
    near_parts = []
    for part in basis_parts:
        near_part = ordered(product, tiles[0], part[:half_marks])
        near_parts.append(ordered(far_product, tiles[1], part[half_marks:], near_part))
    mark_arrived(2)
    mark_arrived(3)
    add_tile(mark_halves[:2], mark_others[:2])
    far_basis[0] = arrived(far_basis[0])
    add_tile(mark_halves[2:], mark_others[2:])
    near_tiles, far_tiles = tiles[:2], tiles[2:]
    stats = jnp.concatenate(tile_stats, 1)
    near, far, across = (lax.ppermute(stats, "dp", swap) for swap in (SWAP_NEAR, SWAP_FAR, ACROSS))
    stats = ordered(joined, joined(stats, near), joined(far, across))
    far_basis[1] = arrived(far_basis[1])
    stats = after(stats, far_basis[1])
    stats = joined(stats, over_y(jnp.concatenate([stats[:, marks:], stats[:, :marks]], 1)))
    sums = [stats[:1, :marks], stats[:1, marks:]]
    peaks = stats[1:].reshape(4, half_marks, 1)

    def centred_of(near_basis, near_part, far_basis):
        part = (
            near_part
            + product(far_tiles[0], far_basis[:half_marks])
            + product(far_tiles[1], far_basis[half_marks:])
        )
        turned = jnp.concatenate([part[data.shape[0] :], part[: data.shape[0]]], 0)
        projected = part + over_cores(turned)
        weighed = weighted_rows(sums[0], near_basis) + weighted_rows(sums[1], far_basis)
        weighed = weighed + over_cores(weighed)
        centred = (projected - weighed[:1] / total_rows).astype(jnp.bfloat16)
        return centred, 2.0**14 / (1.02 * jnp.maximum(weighed[1:], 1e-30))

    def part_of(tile, peak, pair):
        centred, scale = pair
        part = lax.dot_general(
            tile, centred, (((0,), (0,)), ((), ())), preferred_element_type=jnp.float32
        )
        return part * (scale * (1.0 / peak))

    def send_step(tile, index, pair):
        return as_half(part_of(tile, peaks[2 + index], pair))

    def panel_step(received, index, pair):
        return as_half(part_of(near_tiles[index], peaks[index], pair) + received.astype(jnp.float32))

    def sum_step(received, kept):
        return as_half(kept.astype(jnp.float32) + received.astype(jnp.float32))

    def final_step(given, total, index):
        chosen = jnp.where(inner, total, given).astype(jnp.float32)
        return chosen * (peaks[index] * 2.0**-14)

    def split_step(part):
        middle = part.shape[0] // 2
        top, bottom = part[:middle], part[middle:]
        return jnp.where(second, bottom, top), jnp.where(second, top, bottom)

    def add_step(received, kept):
        return received + kept

    def gather_step(others, kept):
        return jnp.concatenate(
            [jnp.where(second, others, kept), jnp.where(second, kept, others)], 0
        )

    centred = [centred_of(*parts) for parts in zip(basis_parts, near_parts, far_basis)]
    chunks = [(index, pair) for pair in centred for index in range(2)]
    received = [
        over_y(ordered(send_step, far_tiles[index], index, pair)) for index, pair in chunks
    ]
    panels, outers, pairs, crosses, totals, givens, finals = ([None] * 4 for _ in range(7))

    def panel(i):
        panels[i] = ordered(panel_step, received[i], *chunks[i])
        outers[i] = lax.ppermute(panels[i], "dp", TO_INNER)

    def joint(i):
        pairs[i] = ordered(sum_step, outers[i], panels[i])
        crosses[i] = lax.ppermute(pairs[i], "dp", SWAP_INNER)

    def total(i):
        totals[i] = ordered(sum_step, crosses[i], pairs[i])
        givens[i] = lax.ppermute(totals[i], "dp", TO_OUTER)

    def final(i):
        finals[i] = ordered(final_step, givens[i], totals[i], chunks[i][0])

    panel(0)
    panel(1)
    joint(0)
    panel(2)
    joint(1)
    total(0)
    panel(3)
    joint(2)
    total(1)
    joint(3)
    total(2)
    final(0)
    final(1)
    first = jnp.concatenate(finals[:2], 0)
    kept, sent = split_step(ordered(product_of, first, first))
    arriving = over_cores(sent)
    total(3)
    kept = ordered(add_step, arriving, kept)
    arriving = over_y(kept)
    final(2)
    kept = ordered(add_step, arriving, kept)
    arriving = over_cores(kept)
    final(3)
    last = jnp.concatenate(finals[2:], 0)
    last_kept, last_sent = split_step(product_of(last, jnp.concatenate([first, last], 1)))
    last_kept = last_kept + over_cores(last_sent)
    last_arriving = over_y(last_kept)
    first_gram = gather_step(after(arriving, last_kept), kept)
    done, solve = whiten_first(first_gram, first)
    last_arriving = after(last_arriving, done)
    last_kept = last_kept + last_arriving
    last_gram = gather_step(over_cores(last_kept), last_kept)
    return whiten_second(last_gram, last, done, solve, math.sqrt(all_marks))


def solution(mesh):
    in_specs = (
        P(("groups", "blk", "dp"), None),
        P(("groups", "blk"), None),
        P(("groups", "blk"), None),
    )
    out_specs = P(("groups", "blk"), None)
    fits = mesh.shape["blk"] == 4 and mesh.shape["dp"] == 4
    return jax.shard_map(
        body if fits else general_body,
        mesh=mesh,
        in_specs=in_specs,
        out_specs=out_specs,
        check_vma=False,
    )
```

```python
import functools
import math

import jax
import jax.numpy as jnp
from jax import lax
from jax.experimental import pallas as pl
from jax.experimental.pallas import tpu as pltpu
from jax.sharding import PartitionSpec as P

NORM_EPS = 1e-06
BLOCK = 128
PANEL = 8
HIGHEST = lax.Precision.HIGHEST
SWAP_CORE = [(0, 1), (1, 0), (2, 3), (3, 2)]
SWAP_Y = [(0, 2), (2, 0), (1, 3), (3, 1)]
SWAP_INNER = [(1, 2), (2, 1)]
TO_INNER = [(0, 1), (3, 2)]
TO_OUTER = [(1, 0), (2, 3)]
SWAP_NEAR = [(0, 1), (1, 0), (2, 3), (3, 2)]
ACROSS = [(0, 3), (3, 0), (1, 2), (2, 1)]
SWAP_FAR = [(0, 2), (2, 0), (1, 3), (3, 1)]


def unit_rows(values):
    wide = values.astype(jnp.float32)
    return (wide * lax.rsqrt(jnp.sum(wide * wide, axis=1, keepdims=True) + NORM_EPS)).astype(
        jnp.bfloat16
    )


def kernel_tile(unit_data, unit_marks, exponent_scale):
    scores = lax.dot_general(
        unit_data, unit_marks, (((1,), (1,)), ((), ())), preferred_element_type=jnp.float32
    )
    return jnp.exp(exponent_scale * scores).astype(jnp.bfloat16)


def spread_row(tile, row):
    return jnp.broadcast_to(tile[row : row + 1, :], tile.shape)


def eliminate_panel(square_ref, inverse_ref, panel, low, high):
    size = square_ref.shape[0]
    lane = lax.broadcasted_iota(jnp.int32, (PANEL, size), 1)
    sublane = lax.broadcasted_iota(jnp.int32, (PANEL, size), 0)
    here = pl.ds(pl.multiple_of(panel * PANEL, PANEL), PANEL)

    def columns_of(rows):
        return [jnp.broadcast_to(rows[:, k : k + 1], (PANEL, size)) for k in range(PANEL)]

    head = square_ref[here, :]
    head_columns = columns_of(head)
    scaled, ratios, finished = [], [], jnp.zeros_like(head)
    for k in range(PANEL):
        pivot = spread_row(head_columns[k], k)
        inverse = 1.0 / pivot
        row = jnp.where(lane == k, 1.0, spread_row(head, k))
        finished = jnp.where(sublane == k, row * lax.rsqrt(pivot), finished)
        scaled.append(row * inverse)
        ratios.append({m: spread_row(head_columns[k], m) * inverse for m in range(k + 1, PANEL)})
        for m in range(k + 1, PANEL):
            head_columns[m] = head_columns[m] - head_columns[k] * ratios[k][m]
        head = jnp.where(lane == k, 0.0, head) - head_columns[k] * scaled[k]
    finished = pltpu.roll(finished, panel * PANEL, 1)
    inverse_ref[here, :] = jnp.where(lane <= panel * PANEL + sublane, finished, 0.0)
    weights = [jnp.where((lane <= k) | (lane >= PANEL), scaled[k], 0.0) for k in range(PANEL)]
    for k in reversed(range(PANEL)):
        for m in range(k + 1, PANEL):
            weights[k] = weights[k] - ratios[k][m] * weights[m]
    for g in range(low, high):
        rows = square_ref[PANEL * g : PANEL * (g + 1), :]
        columns = columns_of(rows)
        rows = jnp.where(lane < PANEL, 0.0, rows)
        for k in range(PANEL):
            rows = rows - columns[k] * weights[k]
        square_ref[PANEL * g : PANEL * (g + 1), :] = pltpu.roll(rows, size - PANEL, 1)


def lower_inverse(square_ref, inverse_ref):
    groups = square_ref.shape[0] // PANEL
    spans = 4

    for low in range(0, groups, groups // spans):

        def step(panel, carry):
            eliminate_panel(square_ref, inverse_ref, panel, low, groups)
            return carry

        lax.fori_loop(low, low + groups // spans, step, 0)


def times_transposed(left, right):
    return lax.dot_general(
        left,
        right,
        (((1,), (1,)), ((), ())),
        precision=HIGHEST,
        preferred_element_type=jnp.float32,
    )


def eliminate(scale, left_ref, rows_ref, inverse_ref, square_ref, write):
    order = left_ref.shape[0]
    blocks = order // BLOCK

    def step(position, carry):
        here = pl.ds(pl.multiple_of(position * BLOCK, BLOCK), BLOCK)
        square_ref[...] = left_ref[here, here]
        lower_inverse(square_ref, inverse_ref)
        for b in range(blocks):

            @pl.when(position == b)
            def _():
                now = slice(b * BLOCK, (b + 1) * BLOCK)
                later = slice((b + 1) * BLOCK, order)
                inverse = inverse_ref[...]
                solved = times_transposed(rows_ref[:, now], inverse)
                if b + 1 < blocks:
                    factor = times_transposed(left_ref[later, now], inverse)
                    left_ref[later, later] -= times_transposed(factor, factor)
                    rows_ref[:, later] -= times_transposed(solved, factor)
                write(now, solved * scale)

        return carry

    lax.fori_loop(0, blocks, step, 0)


def whiten_kernel(scale, gram_ref, rows_ref, out_ref, left_ref, moved_ref, inverse_ref, square_ref):
    left_ref[...] = gram_ref[...]
    moved_ref[...] = rows_ref[...]

    def write(now, values):
        out_ref[:, now] = values

    eliminate(scale, left_ref, moved_ref, inverse_ref, square_ref, write)


def first_kernel(gram_ref, rows_ref, out_ref, back_ref, left_ref, moved_ref, inverse_ref, square_ref):
    count, order = rows_ref.shape
    left_ref[...] = gram_ref[...]
    moved_ref[:count, :] = rows_ref[...]
    shape = (order, order)
    moved_ref[count:, :] = jnp.where(
        lax.broadcasted_iota(jnp.int32, shape, 0) == lax.broadcasted_iota(jnp.int32, shape, 1),
        1.0,
        0.0,
    )

    def write(now, values):
        out_ref[:, now] = values[:count]
        back_ref[:, now] = values[count:]

    eliminate(1.0, left_ref, moved_ref, inverse_ref, square_ref, write)


def second_kernel(
    scale, gram_ref, rows_ref, done_ref, solve_ref, out_ref, left_ref, moved_ref, inverse_ref, square_ref
):
    order = rows_ref.shape[1]
    factor = lax.dot_general(
        gram_ref[:, :order],
        solve_ref[...],
        (((1,), (0,)), ((), ())),
        precision=HIGHEST,
        preferred_element_type=jnp.float32,
    )
    left_ref[...] = gram_ref[:, order:] - times_transposed(factor, factor)
    moved_ref[...] = rows_ref[...] - times_transposed(done_ref[...], factor)
    out_ref[:, :order] = done_ref[...] * scale

    def write(now, values):
        out_ref[:, order + now.start : order + now.stop] = values

    eliminate(scale, left_ref, moved_ref, inverse_ref, square_ref, write)


def solve_call(kernel, out_shapes, moved_shape, *operands):
    vmem = pl.BlockSpec(memory_space=pltpu.VMEM)
    single = len(out_shapes) == 1
    shapes = [jax.ShapeDtypeStruct(shape, jnp.float32) for shape in out_shapes]
    order = moved_shape[1]
    return pl.pallas_call(
        kernel,
        out_shape=shapes[0] if single else shapes,
        in_specs=[vmem] * len(operands),
        out_specs=vmem if single else [vmem] * len(shapes),
        scratch_shapes=[
            pltpu.VMEM((order, order), jnp.float32),
            pltpu.VMEM(moved_shape, jnp.float32),
            pltpu.VMEM((BLOCK, BLOCK), jnp.float32),
            pltpu.VMEM((BLOCK, BLOCK), jnp.float32),
        ],
        compiler_params=pltpu.CompilerParams(vmem_limit_bytes=32 * 2**20),
        cost_estimate=pl.CostEstimate(
            flops=160 * moved_shape[0] * order * order,
            bytes_accessed=4 * moved_shape[0] * order,
            transcendentals=0,
        ),
    )(*operands)


def whiten(gram_matrix, rows, scale):
    kernel = functools.partial(whiten_kernel, scale)
    return solve_call(kernel, [rows.shape], rows.shape, gram_matrix, rows)


def whiten_first(gram_matrix, rows):
    count, order = rows.shape
    return solve_call(
        first_kernel, [rows.shape, (order, order)], (count + order, order), gram_matrix, rows
    )


def whiten_second(gram_rows, rows, done, solve, scale):
    count, order = rows.shape
    kernel = functools.partial(second_kernel, scale)
    return solve_call(
        kernel, [(count, 2 * order)], rows.shape, gram_rows, rows, done, solve
    )


def own_gram(rows):
    return lax.dot_general(rows, rows, (((0,), (0,)), ((), ())), precision=HIGHEST)


def general_body(data, landmarks, basis):
    exponent_scale = math.sqrt(data.shape[1])
    all_marks = landmarks.shape[0] * lax.axis_size("blk")
    total_rows = data.shape[0] * lax.axis_size("blk") * lax.axis_size("dp")
    tile = kernel_tile(
        unit_rows(data),
        lax.all_gather(unit_rows(landmarks), "blk", axis=0, tiled=True),
        exponent_scale,
    )
    projected = jnp.dot(
        tile, lax.all_gather(basis, "blk", axis=0, tiled=True), preferred_element_type=jnp.float32
    )
    column_sums = lax.psum(lax.psum(jnp.sum(projected, axis=0), "blk"), "dp")
    centred = (projected - column_sums / total_rows).astype(jnp.bfloat16)
    partial = lax.dot_general(
        tile, centred, (((0,), (0,)), ((), ())), preferred_element_type=jnp.float32
    )
    panel = lax.psum_scatter(partial, "blk", scatter_dimension=0, tiled=True)
    shares = lax.psum_scatter(panel, "dp", scatter_dimension=0, tiled=True)
    gram_matrix = lax.psum(own_gram(shares), ("blk", "dp"))
    local_rows = whiten(gram_matrix, shares, math.sqrt(all_marks))
    return lax.all_gather(local_rows, "dp", axis=0, tiled=True)


def tile_kernel(exponent_scale, split, data_ref, odd_ref, *refs):
    half_refs, other_refs = refs[:split], refs[split:-3]
    tile_ref, stats_ref, unit_ref = refs[-3:]
    at = 0
    if other_refs:
        odd = odd_ref[0] == 1
        for half_ref, other_ref in zip(half_refs, other_refs):
            count, width = half_ref.shape
            here = slice(at, at + count)
            for low in (True, False):
                span = slice(0, width) if low else slice(width, 2 * width)

                @pl.when(odd == low)
                def _():
                    unit_ref[here, span] = other_ref[...]

                @pl.when(odd != low)
                def _():
                    unit_ref[here, span] = half_ref[...]

            at += count
        unit_ref[...] = unit_rows(unit_ref[...])
    else:
        unit_ref[...] = unit_rows(half_refs[0][...])
    rows = data_ref.shape[0]
    step = math.gcd(rows, 480)

    def add_rows(index, stats):
        here = pl.ds(pl.multiple_of(index * step, step), step)
        scores = lax.dot_general(
            data_ref[here, :],
            unit_ref[...],
            (((1,), (1,)), ((), ())),
            preferred_element_type=jnp.float32,
        )
        tile = jnp.exp(exponent_scale * scores).astype(jnp.bfloat16)
        tile_ref[here, :] = tile
        wide = tile.astype(jnp.float32)
        return stats[0] + jnp.sum(wide, axis=0, keepdims=True), stats[1] + jnp.sum(
            wide * wide, axis=0, keepdims=True
        )

    none = jnp.zeros((1, unit_ref.shape[0]), jnp.float32)
    stats_ref[...] = jnp.concatenate(lax.fori_loop(0, rows // step, add_rows, (none, none), unroll=2), 0)


def tile_call(unit_data, odd, halves, others, exponent_scale):
    vmem = pl.BlockSpec(memory_space=pltpu.VMEM)
    rows, depth = unit_data.shape
    count = sum(half.shape[0] for half in halves)
    return pl.pallas_call(
        functools.partial(tile_kernel, exponent_scale, len(halves)),
        out_shape=[
            jax.ShapeDtypeStruct((rows, count), jnp.bfloat16),
            jax.ShapeDtypeStruct((2, count), jnp.float32),
        ],
        in_specs=[vmem, pl.BlockSpec(memory_space=pltpu.SMEM)] + [vmem] * (len(halves) + len(others)),
        out_specs=[vmem, vmem],
        scratch_shapes=[pltpu.VMEM((count, depth), jnp.bfloat16)],
        compiler_params=pltpu.CompilerParams(vmem_limit_bytes=32 * 2**20),
        cost_estimate=pl.CostEstimate(
            flops=2 * rows * count * depth,
            bytes_accessed=2 * rows * (count + depth),
            transcendentals=rows * count,
        ),
    )(unit_data, odd, *halves, *others)


def over_cores(values):
    return lax.ppermute(values, "blk", SWAP_CORE)


def over_y(values):
    return lax.ppermute(values, "blk", SWAP_Y)


def after(values, *others):
    return lax.optimization_barrier((values, *others))[0]


def product_of(left, right):
    return lax.dot_general(left, right, (((0,), (0,)), ((), ())), precision=HIGHEST)


def product(left, right):
    return jnp.dot(left, right, preferred_element_type=jnp.float32)


def weigh_kernel(stats_ref, near_ref, first_ref, last_ref, out_ref):
    count, width = first_ref.shape

    def split(weights):
        top = weights.astype(jnp.bfloat16).astype(jnp.float32)
        middle = (weights - top).astype(jnp.bfloat16).astype(jnp.float32)
        low = weights - top - middle
        row = lax.broadcasted_iota(jnp.int32, (8, count), 0)
        parts = jnp.where(row == 0, top, jnp.where(row == 1, middle, jnp.where(row == 2, low, 0.0)))
        return parts.astype(jnp.bfloat16)

    near, far = split(stats_ref[:1, :count]), split(stats_ref[:1, count:])
    for index, far_ref in enumerate((first_ref, last_ref)):
        span = slice(index * width, (index + 1) * width)
        near_rows, far_rows = near_ref[:, span], far_ref[...]
        value = jnp.sum(product(near, near_rows), axis=0, keepdims=True) + jnp.sum(
            product(far, far_rows), axis=0, keepdims=True
        )
        size = product(near, jnp.abs(near_rows)) + product(far, jnp.abs(far_rows))
        out_ref[:, span] = jnp.concatenate([value, size[:1]], 0)


def weigh_call(stats, near_rows, first_rows, last_rows):
    return pl.pallas_call(
        weigh_kernel,
        out_shape=jax.ShapeDtypeStruct((2, near_rows.shape[1]), jnp.float32),
        in_specs=[pl.BlockSpec(memory_space=pltpu.VMEM)] * 4,
        out_specs=pl.BlockSpec(memory_space=pltpu.VMEM),
        compiler_params=pltpu.CompilerParams(vmem_limit_bytes=16 * 2**20),
    )(stats, near_rows, first_rows, last_rows)


def as_half(values):
    return lax.optimization_barrier(values.astype(jnp.float16))


def body(data, landmarks, basis):
    exponent_scale = math.sqrt(data.shape[1])
    all_marks = landmarks.shape[0] * lax.axis_size("blk")
    total_rows = data.shape[0] * lax.axis_size("blk") * lax.axis_size("dp")
    second = lax.axis_index("blk") % 2 == 1
    place = lax.axis_index("dp")
    odd = place % 2 == 1
    inner = (place == 1) | (place == 2)
    marks = landmarks.shape[0]
    half_marks = marks // 2
    width = basis.shape[1] // 2

    previous = []

    def ordered(step, operand, *others):
        if previous:
            operand = lax.optimization_barrier((operand, previous.pop()))[0]
        value = step(operand, *others)
        previous.append(jax.tree.leaves(value)[0])
        return value

    def own_half(values):
        middle = values.shape[1] // 2
        return jnp.where(odd, values[:, middle:], values[:, :middle])

    def over_near(values):
        return lax.ppermute(values, "dp", SWAP_NEAR)

    basis_parts = [basis[:, :width], basis[:, width:]]
    near_marks = [landmarks[:half_marks], landmarks[half_marks:]]
    first_half = own_half(near_marks[0])
    received = [over_y(first_half)]
    other_data = over_cores(data)
    second_half = own_half(after(near_marks[1], other_data, first_half))
    received.append(over_y(second_half))
    unit_data = unit_rows(jnp.concatenate([after(data, second_half), other_data], 0))
    parity = (place % 2).astype(jnp.int32).reshape(1)
    tiles, tile_stats = [], []

    def add_tile(halves, others=()):
        tile, stats = ordered(
            lambda first: tile_call(unit_data, parity, [first, *halves[1:]], others, exponent_scale),
            halves[0],
        )
        tiles.append(tile)
        tile_stats.append(stats)

    def arrived(values):
        return ordered(lambda value: value, values)

    def mark_arrived(index):
        mark_halves.append(arrived(received[index]))
        mark_others.append(over_near(mark_halves[index]))

    mark_halves, mark_others = [], []
    add_tile([landmarks])
    far_basis = [over_y(after(basis_parts[0], tiles[0]))]
    mark_arrived(0)
    near_parts = [ordered(product, tiles[0], part) for part in basis_parts]
    far_basis.append(over_y(after(basis_parts[1], *near_parts)))
    mark_arrived(1)
    add_tile(mark_halves[:1], mark_others[:1])
    far_basis[0] = arrived(far_basis[0])
    add_tile(mark_halves[1:], mark_others[1:])
    near_tiles = [tiles[0][:, :half_marks], tiles[0][:, half_marks:]]
    far_tiles = tiles[1:]
    stats = jnp.concatenate(tile_stats, 1)
    near, far, across = (lax.ppermute(stats, "dp", swap) for swap in (SWAP_NEAR, SWAP_FAR, ACROSS))
    stats = ordered(lambda *four: (four[0] + four[1]) + (four[2] + four[3]), stats, near, far, across)
    far_basis[1] = arrived(far_basis[1])
    stats = after(stats, far_basis[1])
    stats = stats + over_y(jnp.concatenate([stats[:, marks:], stats[:, :marks]], 1))
    peaks = jnp.sqrt(stats[1:]).reshape(4, half_marks, 1)
    weighed = weigh_call(stats, basis, *far_basis)
    weighed = weighed + over_cores(weighed)
    means = weighed[:1] / total_rows
    scales = 2.0**14 / (1.02 * jnp.maximum(weighed[1:], 1e-30))

    def project(far_rows, near_part):
        return (
            near_part
            + product(far_tiles[0], far_rows[:half_marks])
            + product(far_tiles[1], far_rows[half_marks:])
        )

    def centre(other, part, columns):
        rows = data.shape[0]
        projected = part + jnp.concatenate([other[rows:], other[:rows]], 0)
        return (projected - means[:, columns]).astype(jnp.bfloat16), scales[:, columns]

    def part_of(tile, peak, pair):
        centred, scale = pair
        part = lax.dot_general(
            tile, centred, (((0,), (0,)), ((), ())), preferred_element_type=jnp.float32
        )
        return part * (scale * (1.0 / peak))

    def send_step(tile, index, pair):
        return as_half(part_of(tile, peaks[2 + index], pair))

    def panel_step(received, index, pair):
        return as_half(part_of(near_tiles[index], peaks[index], pair) + received.astype(jnp.float32))

    def sum_step(received, kept):
        return as_half(kept.astype(jnp.float32) + received.astype(jnp.float32))

    def final_step(given, total, index):
        chosen = jnp.where(inner, total, given).astype(jnp.float32)
        return chosen * (peaks[index] * 2.0**-14)

    def split_step(part):
        middle = part.shape[0] // 2
        top, bottom = part[:middle], part[middle:]
        return jnp.where(second, bottom, top), jnp.where(second, top, bottom)

    def add_step(received, kept):
        return received + kept

    def gather_step(others, kept):
        return jnp.concatenate(
            [jnp.where(second, others, kept), jnp.where(second, kept, others)], 0
        )

    spans = [slice(0, width), slice(width, 2 * width)]
    first_part = project(far_basis[0], near_parts[0])
    last_part = project(far_basis[1], near_parts[1])
    last_other = over_cores(after(last_part, means))
    centred = [ordered(centre, over_cores(first_part), first_part, spans[0])]
    chunks = [(0, centred[0]), (1, centred[0])]
    received = [None] * 4

    def send(i):
        index, pair = chunks[i]
        received[i] = over_y(ordered(send_step, far_tiles[index], index, pair))

    panels, outers, pairs, crosses, totals, givens, finals = ([None] * 4 for _ in range(7))

    def panel(i):
        panels[i] = ordered(panel_step, received[i], *chunks[i])
        outers[i] = lax.ppermute(panels[i], "dp", TO_INNER)

    def joint(i):
        pairs[i] = ordered(sum_step, outers[i], panels[i])
        crosses[i] = lax.ppermute(pairs[i], "dp", SWAP_INNER)

    def total(i):
        totals[i] = ordered(sum_step, crosses[i], pairs[i])
        givens[i] = lax.ppermute(totals[i], "dp", TO_OUTER)

    def final(i):
        finals[i] = ordered(final_step, givens[i], totals[i], chunks[i][0])

    send(0)
    send(1)
    centred.append(ordered(centre, last_other, last_part, spans[1]))
    chunks += [(0, centred[1]), (1, centred[1])]
    panel(0)
    send(2)
    panel(1)
    send(3)
    joint(0)
    panel(2)
    joint(1)
    total(0)
    panel(3)
    joint(2)
    total(1)
    joint(3)
    total(2)
    final(0)
    final(1)
    first = jnp.concatenate(finals[:2], 0)
    kept, sent = split_step(ordered(product_of, first, first))
    arriving = over_cores(sent)
    total(3)
    kept = ordered(add_step, arriving, kept)
    arriving = over_y(kept)
    final(2)
    kept = ordered(add_step, arriving, kept)
    arriving = over_cores(kept)
    final(3)
    last = jnp.concatenate(finals[2:], 0)
    last_kept, last_sent = split_step(product_of(last, jnp.concatenate([first, last], 1)))
    last_kept = last_kept + over_cores(last_sent)
    last_arriving = over_y(last_kept)
    first_gram = gather_step(after(arriving, last_kept), kept)
    done, solve = whiten_first(first_gram, first)
    last_arriving = after(last_arriving, done)
    last_kept = last_kept + last_arriving
    last_gram = gather_step(over_cores(last_kept), last_kept)
    return whiten_second(last_gram, last, done, solve, math.sqrt(all_marks))


def solution(mesh):
    in_specs = (
        P(("groups", "blk", "dp"), None),
        P(("groups", "blk"), None),
        P(("groups", "blk"), None),
    )
    out_specs = P(("groups", "blk"), None)
    fits = mesh.shape["blk"] == 4 and mesh.shape["dp"] == 4
    return jax.shard_map(
        body if fits else general_body,
        mesh=mesh,
        in_specs=in_specs,
        out_specs=out_specs,
        check_vma=False,
    )
```

```python
import functools
import math

import jax
import jax.numpy as jnp
from jax import lax
from jax.experimental import pallas as pl
from jax.experimental.pallas import tpu as pltpu
from jax.sharding import PartitionSpec as P

NORM_EPS = 1e-06
BLOCK = 128
PANEL = 8
HIGHEST = lax.Precision.HIGHEST
SWAP_CORE = [(0, 1), (1, 0), (2, 3), (3, 2)]
SWAP_Y = [(0, 2), (2, 0), (1, 3), (3, 1)]
SWAP_INNER = [(1, 2), (2, 1)]
TO_INNER = [(0, 1), (3, 2)]
TO_OUTER = [(1, 0), (2, 3)]
SWAP_NEAR = [(0, 1), (1, 0), (2, 3), (3, 2)]
ACROSS = [(0, 3), (3, 0), (1, 2), (2, 1)]
SWAP_FAR = [(0, 2), (2, 0), (1, 3), (3, 1)]


def unit_rows(values):
    wide = values.astype(jnp.float32)
    return (wide * lax.rsqrt(jnp.sum(wide * wide, axis=1, keepdims=True) + NORM_EPS)).astype(
        jnp.bfloat16
    )


def kernel_tile(unit_data, unit_marks, exponent_scale):
    scores = lax.dot_general(
        unit_data, unit_marks, (((1,), (1,)), ((), ())), preferred_element_type=jnp.float32
    )
    return jnp.exp(exponent_scale * scores).astype(jnp.bfloat16)


def spread_row(tile, row):
    return jnp.broadcast_to(tile[row : row + 1, :], tile.shape)


def eliminate_panel(square_ref, inverse_ref, panel, low, high):
    size = square_ref.shape[0]
    lane = lax.broadcasted_iota(jnp.int32, (PANEL, size), 1)
    sublane = lax.broadcasted_iota(jnp.int32, (PANEL, size), 0)
    here = pl.ds(pl.multiple_of(panel * PANEL, PANEL), PANEL)

    def columns_of(rows):
        return [jnp.broadcast_to(rows[:, k : k + 1], (PANEL, size)) for k in range(PANEL)]

    head = square_ref[here, :]
    head_columns = columns_of(head)
    scaled, ratios, finished = [], [], jnp.zeros_like(head)
    for k in range(PANEL):
        pivot = spread_row(head_columns[k], k)
        inverse = 1.0 / pivot
        row = jnp.where(lane == k, 1.0, spread_row(head, k))
        finished = jnp.where(sublane == k, row * lax.rsqrt(pivot), finished)
        scaled.append(row * inverse)
        ratios.append({m: spread_row(head_columns[k], m) * inverse for m in range(k + 1, PANEL)})
        for m in range(k + 1, PANEL):
            head_columns[m] = head_columns[m] - head_columns[k] * ratios[k][m]
        head = jnp.where(lane == k, 0.0, head) - head_columns[k] * scaled[k]
    finished = pltpu.roll(finished, panel * PANEL, 1)
    inverse_ref[here, :] = jnp.where(lane <= panel * PANEL + sublane, finished, 0.0)
    weights = [jnp.where((lane <= k) | (lane >= PANEL), scaled[k], 0.0) for k in range(PANEL)]
    for k in reversed(range(PANEL)):
        for m in range(k + 1, PANEL):
            weights[k] = weights[k] - ratios[k][m] * weights[m]
    for g in range(low, high):
        rows = square_ref[PANEL * g : PANEL * (g + 1), :]
        columns = columns_of(rows)
        rows = jnp.where(lane < PANEL, 0.0, rows)
        for k in range(PANEL):
            rows = rows - columns[k] * weights[k]
        square_ref[PANEL * g : PANEL * (g + 1), :] = pltpu.roll(rows, size - PANEL, 1)


def lower_inverse(square_ref, inverse_ref):
    groups = square_ref.shape[0] // PANEL
    spans = 8

    for low in range(0, groups, groups // spans):

        def step(panel, carry):
            eliminate_panel(square_ref, inverse_ref, panel, low, groups)
            return carry

        lax.fori_loop(low, low + groups // spans, step, 0)


def times_transposed(left, right):
    return lax.dot_general(
        left,
        right,
        (((1,), (1,)), ((), ())),
        precision=HIGHEST,
        preferred_element_type=jnp.float32,
    )


def eliminate(scale, left_ref, rows_ref, inverse_ref, square_ref, write):
    order = left_ref.shape[0]
    blocks = order // BLOCK

    def step(position, carry):
        here = pl.ds(pl.multiple_of(position * BLOCK, BLOCK), BLOCK)
        square_ref[...] = left_ref[here, here]
        lower_inverse(square_ref, inverse_ref)
        for b in range(blocks):

            @pl.when(position == b)
            def _():
                now = slice(b * BLOCK, (b + 1) * BLOCK)
                later = slice((b + 1) * BLOCK, order)
                inverse = inverse_ref[...]
                solved = times_transposed(rows_ref[:, now], inverse)
                if b + 1 < blocks:
                    factor = times_transposed(left_ref[later, now], inverse)
                    left_ref[later, later] -= times_transposed(factor, factor)
                    rows_ref[:, later] -= times_transposed(solved, factor)
                write(now, solved * scale)

        return carry

    lax.fori_loop(0, blocks, step, 0)


def whiten_kernel(scale, gram_ref, rows_ref, out_ref, left_ref, moved_ref, inverse_ref, square_ref):
    left_ref[...] = gram_ref[...]
    moved_ref[...] = rows_ref[...]

    def write(now, values):
        out_ref[:, now] = values

    eliminate(scale, left_ref, moved_ref, inverse_ref, square_ref, write)


def first_kernel(gram_ref, rows_ref, out_ref, back_ref, left_ref, moved_ref, inverse_ref, square_ref):
    count, order = rows_ref.shape
    left_ref[...] = gram_ref[...]
    moved_ref[:count, :] = rows_ref[...]
    shape = (order, order)
    moved_ref[count:, :] = jnp.where(
        lax.broadcasted_iota(jnp.int32, shape, 0) == lax.broadcasted_iota(jnp.int32, shape, 1),
        1.0,
        0.0,
    )

    def write(now, values):
        out_ref[:, now] = values[:count]
        back_ref[:, now] = values[count:]

    eliminate(1.0, left_ref, moved_ref, inverse_ref, square_ref, write)


def second_kernel(
    scale, gram_ref, rows_ref, done_ref, solve_ref, out_ref, left_ref, moved_ref, inverse_ref, square_ref
):
    order = rows_ref.shape[1]
    factor = lax.dot_general(
        gram_ref[:, :order],
        solve_ref[...],
        (((1,), (0,)), ((), ())),
        precision=HIGHEST,
        preferred_element_type=jnp.float32,
    )
    left_ref[...] = gram_ref[:, order:] - times_transposed(factor, factor)
    moved_ref[...] = rows_ref[...] - times_transposed(done_ref[...], factor)
    out_ref[:, :order] = done_ref[...] * scale

    def write(now, values):
        out_ref[:, order + now.start : order + now.stop] = values

    eliminate(scale, left_ref, moved_ref, inverse_ref, square_ref, write)


def solve_call(kernel, out_shapes, moved_shape, *operands):
    vmem = pl.BlockSpec(memory_space=pltpu.VMEM)
    single = len(out_shapes) == 1
    shapes = [jax.ShapeDtypeStruct(shape, jnp.float32) for shape in out_shapes]
    order = moved_shape[1]
    return pl.pallas_call(
        kernel,
        out_shape=shapes[0] if single else shapes,
        in_specs=[vmem] * len(operands),
        out_specs=vmem if single else [vmem] * len(shapes),
        scratch_shapes=[
            pltpu.VMEM((order, order), jnp.float32),
            pltpu.VMEM(moved_shape, jnp.float32),
            pltpu.VMEM((BLOCK, BLOCK), jnp.float32),
            pltpu.VMEM((BLOCK, BLOCK), jnp.float32),
        ],
        compiler_params=pltpu.CompilerParams(vmem_limit_bytes=32 * 2**20),
        cost_estimate=pl.CostEstimate(
            flops=160 * moved_shape[0] * order * order,
            bytes_accessed=4 * moved_shape[0] * order,
            transcendentals=0,
        ),
    )(*operands)


def whiten(gram_matrix, rows, scale):
    kernel = functools.partial(whiten_kernel, scale)
    return solve_call(kernel, [rows.shape], rows.shape, gram_matrix, rows)


def whiten_first(gram_matrix, rows):
    count, order = rows.shape
    return solve_call(
        first_kernel, [rows.shape, (order, order)], (count + order, order), gram_matrix, rows
    )


def whiten_second(gram_rows, rows, done, solve, scale):
    count, order = rows.shape
    kernel = functools.partial(second_kernel, scale)
    return solve_call(
        kernel, [(count, 2 * order)], rows.shape, gram_rows, rows, done, solve
    )


def own_gram(rows):
    return lax.dot_general(rows, rows, (((0,), (0,)), ((), ())), precision=HIGHEST)


def general_body(data, landmarks, basis):
    exponent_scale = math.sqrt(data.shape[1])
    all_marks = landmarks.shape[0] * lax.axis_size("blk")
    total_rows = data.shape[0] * lax.axis_size("blk") * lax.axis_size("dp")
    tile = kernel_tile(
        unit_rows(data),
        lax.all_gather(unit_rows(landmarks), "blk", axis=0, tiled=True),
        exponent_scale,
    )
    projected = jnp.dot(
        tile, lax.all_gather(basis, "blk", axis=0, tiled=True), preferred_element_type=jnp.float32
    )
    column_sums = lax.psum(lax.psum(jnp.sum(projected, axis=0), "blk"), "dp")
    centred = (projected - column_sums / total_rows).astype(jnp.bfloat16)
    partial = lax.dot_general(
        tile, centred, (((0,), (0,)), ((), ())), preferred_element_type=jnp.float32
    )
    panel = lax.psum_scatter(partial, "blk", scatter_dimension=0, tiled=True)
    shares = lax.psum_scatter(panel, "dp", scatter_dimension=0, tiled=True)
    gram_matrix = lax.psum(own_gram(shares), ("blk", "dp"))
    local_rows = whiten(gram_matrix, shares, math.sqrt(all_marks))
    return lax.all_gather(local_rows, "dp", axis=0, tiled=True)


def tile_kernel(exponent_scale, split, data_ref, odd_ref, *refs):
    half_refs, other_refs = refs[:split], refs[split:-3]
    tile_ref, stats_ref, unit_ref = refs[-3:]
    at = 0
    if other_refs:
        odd = odd_ref[0] == 1
        for half_ref, other_ref in zip(half_refs, other_refs):
            count, width = half_ref.shape
            here = slice(at, at + count)
            for low in (True, False):
                span = slice(0, width) if low else slice(width, 2 * width)

                @pl.when(odd == low)
                def _():
                    unit_ref[here, span] = other_ref[...]

                @pl.when(odd != low)
                def _():
                    unit_ref[here, span] = half_ref[...]

            at += count
        unit_ref[...] = unit_rows(unit_ref[...])
    else:
        unit_ref[...] = unit_rows(half_refs[0][...])
    rows = data_ref.shape[0]
    step = math.gcd(rows, 480)

    def add_rows(index, stats):
        here = pl.ds(pl.multiple_of(index * step, step), step)
        scores = lax.dot_general(
            data_ref[here, :],
            unit_ref[...],
            (((1,), (1,)), ((), ())),
            preferred_element_type=jnp.float32,
        )
        tile = jnp.exp(exponent_scale * scores).astype(jnp.bfloat16)
        tile_ref[here, :] = tile
        wide = tile.astype(jnp.float32)
        return stats[0] + jnp.sum(wide, axis=0, keepdims=True), stats[1] + jnp.sum(
            wide * wide, axis=0, keepdims=True
        )

    none = jnp.zeros((1, unit_ref.shape[0]), jnp.float32)
    stats_ref[...] = jnp.concatenate(lax.fori_loop(0, rows // step, add_rows, (none, none), unroll=2), 0)


def tile_call(unit_data, odd, halves, others, exponent_scale):
    vmem = pl.BlockSpec(memory_space=pltpu.VMEM)
    rows, depth = unit_data.shape
    count = sum(half.shape[0] for half in halves)
    return pl.pallas_call(
        functools.partial(tile_kernel, exponent_scale, len(halves)),
        out_shape=[
            jax.ShapeDtypeStruct((rows, count), jnp.bfloat16),
            jax.ShapeDtypeStruct((2, count), jnp.float32),
        ],
        in_specs=[vmem, pl.BlockSpec(memory_space=pltpu.SMEM)] + [vmem] * (len(halves) + len(others)),
        out_specs=[vmem, vmem],
        scratch_shapes=[pltpu.VMEM((count, depth), jnp.bfloat16)],
        compiler_params=pltpu.CompilerParams(vmem_limit_bytes=32 * 2**20),
        cost_estimate=pl.CostEstimate(
            flops=2 * rows * count * depth,
            bytes_accessed=2 * rows * (count + depth),
            transcendentals=rows * count,
        ),
    )(unit_data, odd, *halves, *others)


def over_cores(values):
    return lax.ppermute(values, "blk", SWAP_CORE)


def over_y(values):
    return lax.ppermute(values, "blk", SWAP_Y)


def after(values, *others):
    return lax.optimization_barrier((values, *others))[0]


def product_of(left, right):
    return lax.dot_general(left, right, (((0,), (0,)), ((), ())), precision=HIGHEST)


def product(left, right):
    return jnp.dot(left, right, preferred_element_type=jnp.float32)


def weigh_kernel(stats_ref, near_ref, first_ref, last_ref, out_ref):
    count, width = first_ref.shape

    def split(weights):
        top = weights.astype(jnp.bfloat16).astype(jnp.float32)
        middle = (weights - top).astype(jnp.bfloat16).astype(jnp.float32)
        low = weights - top - middle
        row = lax.broadcasted_iota(jnp.int32, (8, count), 0)
        parts = jnp.where(row == 0, top, jnp.where(row == 1, middle, jnp.where(row == 2, low, 0.0)))
        return parts.astype(jnp.bfloat16)

    near, far = split(stats_ref[:1, :count]), split(stats_ref[:1, count:])
    for index, far_ref in enumerate((first_ref, last_ref)):
        span = slice(index * width, (index + 1) * width)
        near_rows, far_rows = near_ref[:, span], far_ref[...]
        value = jnp.sum(product(near, near_rows), axis=0, keepdims=True) + jnp.sum(
            product(far, far_rows), axis=0, keepdims=True
        )
        size = product(near, jnp.abs(near_rows)) + product(far, jnp.abs(far_rows))
        out_ref[:, span] = jnp.concatenate([value, size[:1]], 0)


def weigh_call(stats, near_rows, first_rows, last_rows):
    return pl.pallas_call(
        weigh_kernel,
        out_shape=jax.ShapeDtypeStruct((2, near_rows.shape[1]), jnp.float32),
        in_specs=[pl.BlockSpec(memory_space=pltpu.VMEM)] * 4,
        out_specs=pl.BlockSpec(memory_space=pltpu.VMEM),
        compiler_params=pltpu.CompilerParams(vmem_limit_bytes=16 * 2**20),
    )(stats, near_rows, first_rows, last_rows)


def gram_kernel(upper_ref, lower_ref, out_ref):
    upper, lower = upper_ref[...], lower_ref[...]
    out_ref[...] = product_of(upper, upper) + product_of(lower, lower)


def gram_call(upper, lower):
    rows, order = upper.shape
    vmem = pl.BlockSpec(memory_space=pltpu.VMEM)
    return pl.pallas_call(
        gram_kernel,
        out_shape=jax.ShapeDtypeStruct((order, order), jnp.float32),
        in_specs=[vmem, vmem],
        out_specs=vmem,
        compiler_params=pltpu.CompilerParams(vmem_limit_bytes=16 * 2**20),
        cost_estimate=pl.CostEstimate(
            flops=24 * rows * order * order, bytes_accessed=8 * rows * order, transcendentals=0
        ),
    )(upper, lower)


def as_half(values):
    return lax.optimization_barrier(values.astype(jnp.float16))


def body(data, landmarks, basis):
    exponent_scale = math.sqrt(data.shape[1])
    all_marks = landmarks.shape[0] * lax.axis_size("blk")
    total_rows = data.shape[0] * lax.axis_size("blk") * lax.axis_size("dp")
    second = lax.axis_index("blk") % 2 == 1
    place = lax.axis_index("dp")
    odd = place % 2 == 1
    inner = (place == 1) | (place == 2)
    marks = landmarks.shape[0]
    half_marks = marks // 2
    width = basis.shape[1] // 2

    previous = []

    def ordered(step, operand, *others):
        if previous:
            operand = lax.optimization_barrier((operand, previous.pop()))[0]
        value = step(operand, *others)
        previous.append(jax.tree.leaves(value)[0])
        return value

    def own_half(values):
        middle = values.shape[1] // 2
        return jnp.where(odd, values[:, middle:], values[:, :middle])

    def over_near(values):
        return lax.ppermute(values, "dp", SWAP_NEAR)

    basis_parts = [basis[:, :width], basis[:, width:]]
    near_marks = [landmarks[:half_marks], landmarks[half_marks:]]
    first_half = own_half(near_marks[0])
    received = [over_y(first_half)]
    other_data = over_cores(data)
    second_half = own_half(after(near_marks[1], other_data, first_half))
    received.append(over_y(second_half))
    unit_data = unit_rows(jnp.concatenate([after(data, second_half), other_data], 0))
    parity = (place % 2).astype(jnp.int32).reshape(1)
    tiles, tile_stats = [], []

    def add_tile(halves, others=()):
        tile, stats = ordered(
            lambda first: tile_call(unit_data, parity, [first, *halves[1:]], others, exponent_scale),
            halves[0],
        )
        tiles.append(tile)
        tile_stats.append(stats)

    def arrived(values):
        return ordered(lambda value: value, values)

    def mark_arrived(index):
        mark_halves.append(arrived(received[index]))
        mark_others.append(over_near(mark_halves[index]))

    mark_halves, mark_others = [], []
    add_tile([landmarks])
    far_basis = [over_y(after(basis_parts[0], tiles[0]))]
    mark_arrived(0)
    near_parts = [ordered(product, tiles[0], part) for part in basis_parts]
    far_basis.append(over_y(after(basis_parts[1], *near_parts)))
    mark_arrived(1)
    add_tile(mark_halves[:1], mark_others[:1])
    far_basis[0] = arrived(far_basis[0])
    add_tile(mark_halves[1:], mark_others[1:])
    near_tiles = [tiles[0][:, :half_marks], tiles[0][:, half_marks:]]
    far_tiles = tiles[1:]
    stats = jnp.concatenate(tile_stats, 1)
    near, far, across = (lax.ppermute(stats, "dp", swap) for swap in (SWAP_NEAR, SWAP_FAR, ACROSS))
    stats = ordered(lambda *four: (four[0] + four[1]) + (four[2] + four[3]), stats, near, far, across)
    far_basis[1] = arrived(far_basis[1])
    stats = after(stats, far_basis[1])
    stats = stats + over_y(jnp.concatenate([stats[:, marks:], stats[:, :marks]], 1))
    peaks = jnp.sqrt(stats[1:]).reshape(4, half_marks, 1)
    weighed = weigh_call(stats, basis, *far_basis)
    weighed = weighed + over_cores(weighed)
    means = weighed[:1] / total_rows
    scales = 2.0**14 / (1.02 * jnp.maximum(weighed[1:], 1e-30))

    def project(far_rows, near_part):
        return (
            near_part
            + product(far_tiles[0], far_rows[:half_marks])
            + product(far_tiles[1], far_rows[half_marks:])
        )

    def centre(other, part, columns):
        rows = data.shape[0]
        projected = part + jnp.concatenate([other[rows:], other[:rows]], 0)
        return (projected - means[:, columns]).astype(jnp.bfloat16), scales[:, columns]

    def part_of(tile, peak, pair):
        centred, scale = pair
        part = lax.dot_general(
            tile, centred, (((0,), (0,)), ((), ())), preferred_element_type=jnp.float32
        )
        return part * (scale * (1.0 / peak))

    def send_step(tile, index, pair):
        return as_half(part_of(tile, peaks[2 + index], pair))

    def panel_step(received, index, pair):
        return as_half(part_of(near_tiles[index], peaks[index], pair) + received.astype(jnp.float32))

    def sum_step(received, kept):
        return as_half(kept.astype(jnp.float32) + received.astype(jnp.float32))

    def final_step(given, total, index):
        chosen = jnp.where(inner, total, given).astype(jnp.float32)
        return chosen * (peaks[index] * 2.0**-14)

    def split_step(part):
        middle = part.shape[0] // 2
        top, bottom = part[:middle], part[middle:]
        return jnp.where(second, bottom, top), jnp.where(second, top, bottom)

    def add_step(received, kept):
        return received + kept

    def gather_step(others, kept):
        return jnp.concatenate(
            [jnp.where(second, others, kept), jnp.where(second, kept, others)], 0
        )

    spans = [slice(0, width), slice(width, 2 * width)]
    first_part = project(far_basis[0], near_parts[0])
    last_part = project(far_basis[1], near_parts[1])
    last_other = over_cores(after(last_part, means))
    centred = [ordered(centre, over_cores(first_part), first_part, spans[0])]
    chunks = [(0, centred[0]), (1, centred[0])]
    received = [None] * 4

    def send(i):
        index, pair = chunks[i]
        received[i] = over_y(ordered(send_step, far_tiles[index], index, pair))

    panels, outers, pairs, crosses, totals, givens, finals = ([None] * 4 for _ in range(7))

    def panel(i):
        panels[i] = ordered(panel_step, received[i], *chunks[i])
        outers[i] = lax.ppermute(panels[i], "dp", TO_INNER)

    def joint(i):
        pairs[i] = ordered(sum_step, outers[i], panels[i])
        crosses[i] = lax.ppermute(pairs[i], "dp", SWAP_INNER)

    def total(i):
        totals[i] = ordered(sum_step, crosses[i], pairs[i])
        givens[i] = lax.ppermute(totals[i], "dp", TO_OUTER)

    def final(i):
        finals[i] = ordered(final_step, givens[i], totals[i], chunks[i][0])

    send(0)
    send(1)
    centred.append(ordered(centre, last_other, last_part, spans[1]))
    chunks += [(0, centred[1]), (1, centred[1])]
    panel(0)
    send(2)
    panel(1)
    send(3)
    joint(0)
    panel(2)
    joint(1)
    total(0)
    panel(3)
    joint(2)
    total(1)
    joint(3)
    total(2)
    final(0)
    final(1)
    first = jnp.concatenate(finals[:2], 0)
    kept, sent = split_step(ordered(gram_call, *finals[:2]))
    arriving = over_cores(sent)
    total(3)
    kept = ordered(add_step, arriving, kept)
    arriving = over_y(kept)
    final(2)
    kept = ordered(add_step, arriving, kept)
    arriving = over_cores(kept)
    final(3)
    last = jnp.concatenate(finals[2:], 0)
    last_kept, last_sent = split_step(product_of(last, jnp.concatenate([first, last], 1)))
    last_kept = last_kept + over_cores(last_sent)
    last_arriving = over_y(last_kept)
    first_gram = gather_step(after(arriving, last_kept), kept)
    done, solve = whiten_first(first_gram, first)
    last_arriving = after(last_arriving, done)
    last_kept = last_kept + last_arriving
    last_gram = gather_step(over_cores(last_kept), last_kept)
    return whiten_second(last_gram, last, done, solve, math.sqrt(all_marks))


def solution(mesh):
    in_specs = (
        P(("groups", "blk", "dp"), None),
        P(("groups", "blk"), None),
        P(("groups", "blk"), None),
    )
    out_specs = P(("groups", "blk"), None)
    fits = mesh.shape["blk"] == 4 and mesh.shape["dp"] == 4
    return jax.shard_map(
        body if fits else general_body,
        mesh=mesh,
        in_specs=in_specs,
        out_specs=out_specs,
        check_vma=False,
    )
```

```python
import functools
import math

import jax
import jax.numpy as jnp
from jax import lax
from jax.experimental import pallas as pl
from jax.experimental.pallas import tpu as pltpu
from jax.sharding import PartitionSpec as P

NORM_EPS = 1e-06
BLOCK = 128
PANEL = 8
HIGHEST = lax.Precision.HIGHEST
SWAP_CORE = [(0, 1), (1, 0), (2, 3), (3, 2)]
SWAP_Y = [(0, 2), (2, 0), (1, 3), (3, 1)]
SWAP_INNER = [(1, 2), (2, 1)]
TO_INNER = [(0, 1), (3, 2)]
TO_OUTER = [(1, 0), (2, 3)]
SWAP_NEAR = [(0, 1), (1, 0), (2, 3), (3, 2)]
ACROSS = [(0, 3), (3, 0), (1, 2), (2, 1)]
SWAP_FAR = [(0, 2), (2, 0), (1, 3), (3, 1)]


def unit_rows(values):
    wide = values.astype(jnp.float32)
    return (wide * lax.rsqrt(jnp.sum(wide * wide, axis=1, keepdims=True) + NORM_EPS)).astype(
        jnp.bfloat16
    )


def kernel_tile(unit_data, unit_marks, exponent_scale):
    scores = lax.dot_general(
        unit_data, unit_marks, (((1,), (1,)), ((), ())), preferred_element_type=jnp.float32
    )
    return jnp.exp(exponent_scale * scores).astype(jnp.bfloat16)


def spread_row(tile, row):
    return jnp.broadcast_to(tile[row : row + 1, :], tile.shape)


def eliminate_panel(square_ref, inverse_ref, panel, low, high):
    size = square_ref.shape[0]
    lane = lax.broadcasted_iota(jnp.int32, (PANEL, size), 1)
    sublane = lax.broadcasted_iota(jnp.int32, (PANEL, size), 0)
    here = pl.ds(pl.multiple_of(panel * PANEL, PANEL), PANEL)

    def columns_of(rows):
        return [jnp.broadcast_to(rows[:, k : k + 1], (PANEL, size)) for k in range(PANEL)]

    head = square_ref[here, :]
    head_columns = columns_of(head)
    scaled, ratios, finished = [], [], jnp.zeros_like(head)
    for k in range(PANEL):
        pivot = spread_row(head_columns[k], k)
        inverse = 1.0 / pivot
        row = jnp.where(lane == k, 1.0, spread_row(head, k))
        finished = jnp.where(sublane == k, row * lax.rsqrt(pivot), finished)
        scaled.append(row * inverse)
        ratios.append({m: spread_row(head_columns[k], m) * inverse for m in range(k + 1, PANEL)})
        for m in range(k + 1, PANEL):
            head_columns[m] = head_columns[m] - head_columns[k] * ratios[k][m]
        head = jnp.where(lane == k, 0.0, head) - head_columns[k] * scaled[k]
    finished = pltpu.roll(finished, panel * PANEL, 1)
    inverse_ref[here, :] = jnp.where(lane <= panel * PANEL + sublane, finished, 0.0)
    weights = [jnp.where((lane <= k) | (lane >= PANEL), scaled[k], 0.0) for k in range(PANEL)]
    for k in reversed(range(PANEL)):
        for m in range(k + 1, PANEL):
            weights[k] = weights[k] - ratios[k][m] * weights[m]
    for g in range(low, high):
        rows = square_ref[PANEL * g : PANEL * (g + 1), :]
        columns = columns_of(rows)
        rows = jnp.where(lane < PANEL, 0.0, rows)
        for k in range(PANEL):
            rows = rows - columns[k] * weights[k]
        square_ref[PANEL * g : PANEL * (g + 1), :] = pltpu.roll(rows, size - PANEL, 1)


def lower_inverse(square_ref, inverse_ref):
    groups = square_ref.shape[0] // PANEL
    spans = 8

    for low in range(0, groups, groups // spans):

        def step(panel, carry):
            eliminate_panel(square_ref, inverse_ref, panel, low, groups)
            return carry

        lax.fori_loop(low, low + groups // spans, step, 0)


def times_transposed(left, right):
    return lax.dot_general(
        left,
        right,
        (((1,), (1,)), ((), ())),
        precision=HIGHEST,
        preferred_element_type=jnp.float32,
    )


def eliminate(scale, left_ref, rows_ref, inverse_ref, square_ref, write):
    order = left_ref.shape[0]
    blocks = order // BLOCK

    def step(position, carry):
        here = pl.ds(pl.multiple_of(position * BLOCK, BLOCK), BLOCK)
        square_ref[...] = left_ref[here, here]
        lower_inverse(square_ref, inverse_ref)
        for b in range(blocks):

            @pl.when(position == b)
            def _():
                now = slice(b * BLOCK, (b + 1) * BLOCK)
                later = slice((b + 1) * BLOCK, order)
                inverse = inverse_ref[...]
                solved = times_transposed(rows_ref[:, now], inverse)
                if b + 1 < blocks:
                    factor = times_transposed(left_ref[later, now], inverse)
                    left_ref[later, later] -= times_transposed(factor, factor)
                    rows_ref[:, later] -= times_transposed(solved, factor)
                write(now, solved * scale)

        return carry

    lax.fori_loop(0, blocks, step, 0)


def whiten_kernel(scale, gram_ref, rows_ref, out_ref, left_ref, moved_ref, inverse_ref, square_ref):
    left_ref[...] = gram_ref[...]
    moved_ref[...] = rows_ref[...]

    def write(now, values):
        out_ref[:, now] = values

    eliminate(scale, left_ref, moved_ref, inverse_ref, square_ref, write)


def first_kernel(gram_ref, rows_ref, out_ref, back_ref, left_ref, moved_ref, inverse_ref, square_ref):
    count, order = rows_ref.shape
    left_ref[...] = gram_ref[...]
    moved_ref[:count, :] = rows_ref[...]
    shape = (order, order)
    moved_ref[count:, :] = jnp.where(
        lax.broadcasted_iota(jnp.int32, shape, 0) == lax.broadcasted_iota(jnp.int32, shape, 1),
        1.0,
        0.0,
    )

    def write(now, values):
        out_ref[:, now] = values[:count]
        back_ref[:, now] = values[count:]

    eliminate(1.0, left_ref, moved_ref, inverse_ref, square_ref, write)


def second_kernel(
    scale, gram_ref, rows_ref, done_ref, solve_ref, out_ref, left_ref, moved_ref, inverse_ref, square_ref
):
    order = rows_ref.shape[1]
    factor = lax.dot_general(
        gram_ref[:, :order],
        solve_ref[...],
        (((1,), (0,)), ((), ())),
        precision=HIGHEST,
        preferred_element_type=jnp.float32,
    )
    left_ref[...] = gram_ref[:, order:] - times_transposed(factor, factor)
    moved_ref[...] = rows_ref[...] - times_transposed(done_ref[...], factor)
    out_ref[:, :order] = done_ref[...] * scale

    def write(now, values):
        out_ref[:, order + now.start : order + now.stop] = values

    eliminate(scale, left_ref, moved_ref, inverse_ref, square_ref, write)


def solve_call(kernel, out_shapes, moved_shape, *operands):
    vmem = pl.BlockSpec(memory_space=pltpu.VMEM)
    single = len(out_shapes) == 1
    shapes = [jax.ShapeDtypeStruct(shape, jnp.float32) for shape in out_shapes]
    order = moved_shape[1]
    return pl.pallas_call(
        kernel,
        out_shape=shapes[0] if single else shapes,
        in_specs=[vmem] * len(operands),
        out_specs=vmem if single else [vmem] * len(shapes),
        scratch_shapes=[
            pltpu.VMEM((order, order), jnp.float32),
            pltpu.VMEM(moved_shape, jnp.float32),
            pltpu.VMEM((BLOCK, BLOCK), jnp.float32),
            pltpu.VMEM((BLOCK, BLOCK), jnp.float32),
        ],
        compiler_params=pltpu.CompilerParams(vmem_limit_bytes=32 * 2**20),
        cost_estimate=pl.CostEstimate(
            flops=160 * moved_shape[0] * order * order,
            bytes_accessed=4 * moved_shape[0] * order,
            transcendentals=0,
        ),
    )(*operands)


def whiten(gram_matrix, rows, scale):
    kernel = functools.partial(whiten_kernel, scale)
    return solve_call(kernel, [rows.shape], rows.shape, gram_matrix, rows)


def whiten_first(gram_matrix, rows):
    count, order = rows.shape
    return solve_call(
        first_kernel, [rows.shape, (order, order)], (count + order, order), gram_matrix, rows
    )


def whiten_second(gram_rows, rows, done, solve, scale):
    count, order = rows.shape
    kernel = functools.partial(second_kernel, scale)
    return solve_call(
        kernel, [(count, 2 * order)], rows.shape, gram_rows, rows, done, solve
    )


def own_gram(rows):
    return lax.dot_general(rows, rows, (((0,), (0,)), ((), ())), precision=HIGHEST)


def general_body(data, landmarks, basis):
    exponent_scale = math.sqrt(data.shape[1])
    all_marks = landmarks.shape[0] * lax.axis_size("blk")
    total_rows = data.shape[0] * lax.axis_size("blk") * lax.axis_size("dp")
    tile = kernel_tile(
        unit_rows(data),
        lax.all_gather(unit_rows(landmarks), "blk", axis=0, tiled=True),
        exponent_scale,
    )
    projected = jnp.dot(
        tile, lax.all_gather(basis, "blk", axis=0, tiled=True), preferred_element_type=jnp.float32
    )
    column_sums = lax.psum(lax.psum(jnp.sum(projected, axis=0), "blk"), "dp")
    centred = (projected - column_sums / total_rows).astype(jnp.bfloat16)
    partial = lax.dot_general(
        tile, centred, (((0,), (0,)), ((), ())), preferred_element_type=jnp.float32
    )
    panel = lax.psum_scatter(partial, "blk", scatter_dimension=0, tiled=True)
    shares = lax.psum_scatter(panel, "dp", scatter_dimension=0, tiled=True)
    gram_matrix = lax.psum(own_gram(shares), ("blk", "dp"))
    local_rows = whiten(gram_matrix, shares, math.sqrt(all_marks))
    return lax.all_gather(local_rows, "dp", axis=0, tiled=True)


def tile_kernel(exponent_scale, split, data_ref, odd_ref, *refs):
    half_refs, other_refs = refs[:split], refs[split:-3]
    tile_ref, stats_ref, unit_ref = refs[-3:]
    at = 0
    if other_refs:
        odd = odd_ref[0] == 1
        for half_ref, other_ref in zip(half_refs, other_refs):
            count, width = half_ref.shape
            here = slice(at, at + count)
            for low in (True, False):
                span = slice(0, width) if low else slice(width, 2 * width)

                @pl.when(odd == low)
                def _():
                    unit_ref[here, span] = other_ref[...]

                @pl.when(odd != low)
                def _():
                    unit_ref[here, span] = half_ref[...]

            at += count
        unit_ref[...] = unit_rows(unit_ref[...])
    else:
        unit_ref[...] = unit_rows(half_refs[0][...])
    rows = data_ref.shape[0]
    step = math.gcd(rows, 480)

    def add_rows(index, stats):
        here = pl.ds(pl.multiple_of(index * step, step), step)
        scores = lax.dot_general(
            data_ref[here, :],
            unit_ref[...],
            (((1,), (1,)), ((), ())),
            preferred_element_type=jnp.float32,
        )
        tile = jnp.exp(exponent_scale * scores).astype(jnp.bfloat16)
        tile_ref[here, :] = tile
        wide = tile.astype(jnp.float32)
        return stats[0] + jnp.sum(wide, axis=0, keepdims=True), stats[1] + jnp.sum(
            wide * wide, axis=0, keepdims=True
        )

    none = jnp.zeros((1, unit_ref.shape[0]), jnp.float32)
    stats_ref[...] = jnp.concatenate(lax.fori_loop(0, rows // step, add_rows, (none, none), unroll=4 if other_refs else 2), 0)


def tile_call(unit_data, odd, halves, others, exponent_scale):
    vmem = pl.BlockSpec(memory_space=pltpu.VMEM)
    rows, depth = unit_data.shape
    count = sum(half.shape[0] for half in halves)
    return pl.pallas_call(
        functools.partial(tile_kernel, exponent_scale, len(halves)),
        out_shape=[
            jax.ShapeDtypeStruct((rows, count), jnp.bfloat16),
            jax.ShapeDtypeStruct((2, count), jnp.float32),
        ],
        in_specs=[vmem, pl.BlockSpec(memory_space=pltpu.SMEM)] + [vmem] * (len(halves) + len(others)),
        out_specs=[vmem, vmem],
        scratch_shapes=[pltpu.VMEM((count, depth), jnp.bfloat16)],
        compiler_params=pltpu.CompilerParams(vmem_limit_bytes=32 * 2**20),
        cost_estimate=pl.CostEstimate(
            flops=2 * rows * count * depth,
            bytes_accessed=2 * rows * (count + depth),
            transcendentals=rows * count,
        ),
    )(unit_data, odd, *halves, *others)


def over_cores(values):
    return lax.ppermute(values, "blk", SWAP_CORE)


def over_y(values):
    return lax.ppermute(values, "blk", SWAP_Y)


def after(values, *others):
    return lax.optimization_barrier((values, *others))[0]


def product_of(left, right):
    return lax.dot_general(left, right, (((0,), (0,)), ((), ())), precision=HIGHEST)


def product(left, right):
    return jnp.dot(left, right, preferred_element_type=jnp.float32)


def weigh_kernel(stats_ref, near_ref, first_ref, last_ref, out_ref):
    count, width = first_ref.shape

    def split(weights):
        top = weights.astype(jnp.bfloat16).astype(jnp.float32)
        middle = (weights - top).astype(jnp.bfloat16).astype(jnp.float32)
        low = weights - top - middle
        row = lax.broadcasted_iota(jnp.int32, (8, count), 0)
        parts = jnp.where(row == 0, top, jnp.where(row == 1, middle, jnp.where(row == 2, low, 0.0)))
        return parts.astype(jnp.bfloat16)

    near, far = split(stats_ref[:1, :count]), split(stats_ref[:1, count:])
    for index, far_ref in enumerate((first_ref, last_ref)):
        span = slice(index * width, (index + 1) * width)
        near_rows, far_rows = near_ref[:, span], far_ref[...]
        value = jnp.sum(product(near, near_rows), axis=0, keepdims=True) + jnp.sum(
            product(far, far_rows), axis=0, keepdims=True
        )
        size = product(near, jnp.abs(near_rows)) + product(far, jnp.abs(far_rows))
        out_ref[:, span] = jnp.concatenate([value, size[:1]], 0)


def weigh_call(stats, near_rows, first_rows, last_rows):
    return pl.pallas_call(
        weigh_kernel,
        out_shape=jax.ShapeDtypeStruct((2, near_rows.shape[1]), jnp.float32),
        in_specs=[pl.BlockSpec(memory_space=pltpu.VMEM)] * 4,
        out_specs=pl.BlockSpec(memory_space=pltpu.VMEM),
        compiler_params=pltpu.CompilerParams(vmem_limit_bytes=16 * 2**20),
    )(stats, near_rows, first_rows, last_rows)


def gram_kernel(upper_ref, lower_ref, out_ref):
    upper, lower = upper_ref[...], lower_ref[...]
    out_ref[...] = product_of(upper, upper) + product_of(lower, lower)


def gram_call(upper, lower):
    rows, order = upper.shape
    vmem = pl.BlockSpec(memory_space=pltpu.VMEM)
    return pl.pallas_call(
        gram_kernel,
        out_shape=jax.ShapeDtypeStruct((order, order), jnp.float32),
        in_specs=[vmem, vmem],
        out_specs=vmem,
        compiler_params=pltpu.CompilerParams(vmem_limit_bytes=16 * 2**20),
        cost_estimate=pl.CostEstimate(
            flops=24 * rows * order * order, bytes_accessed=8 * rows * order, transcendentals=0
        ),
    )(upper, lower)


def as_half(values):
    return lax.optimization_barrier(values.astype(jnp.float16))


def body(data, landmarks, basis):
    exponent_scale = math.sqrt(data.shape[1])
    all_marks = landmarks.shape[0] * lax.axis_size("blk")
    total_rows = data.shape[0] * lax.axis_size("blk") * lax.axis_size("dp")
    second = lax.axis_index("blk") % 2 == 1
    place = lax.axis_index("dp")
    odd = place % 2 == 1
    inner = (place == 1) | (place == 2)
    marks = landmarks.shape[0]
    half_marks = marks // 2
    width = basis.shape[1] // 2

    previous = []

    def ordered(step, operand, *others):
        if previous:
            operand = lax.optimization_barrier((operand, previous.pop()))[0]
        value = step(operand, *others)
        previous.append(jax.tree.leaves(value)[0])
        return value

    def own_half(values):
        middle = values.shape[1] // 2
        return jnp.where(odd, values[:, middle:], values[:, :middle])

    def over_near(values):
        return lax.ppermute(values, "dp", SWAP_NEAR)

    basis_parts = [basis[:, :width], basis[:, width:]]
    near_marks = [landmarks[:half_marks], landmarks[half_marks:]]
    first_half = own_half(near_marks[0])
    received = [over_y(first_half)]
    other_data = over_cores(data)
    second_half = own_half(after(near_marks[1], other_data, first_half))
    received.append(over_y(second_half))
    unit_data = unit_rows(jnp.concatenate([after(data, second_half), other_data], 0))
    parity = (place % 2).astype(jnp.int32).reshape(1)
    tiles, tile_stats = [], []

    def add_tile(halves, others=()):
        tile, stats = ordered(
            lambda first: tile_call(unit_data, parity, [first, *halves[1:]], others, exponent_scale),
            halves[0],
        )
        tiles.append(tile)
        tile_stats.append(stats)

    def arrived(values):
        return ordered(lambda value: value, values)

    def mark_arrived(index):
        mark_halves.append(arrived(received[index]))
        mark_others.append(over_near(mark_halves[index]))

    mark_halves, mark_others = [], []
    add_tile([landmarks])
    far_basis = [over_y(after(basis_parts[0], tiles[0]))]
    mark_arrived(0)
    near_parts = [ordered(product, tiles[0], part) for part in basis_parts]
    far_basis.append(over_y(after(basis_parts[1], *near_parts)))
    mark_arrived(1)
    add_tile(mark_halves[:1], mark_others[:1])
    far_basis[0] = arrived(far_basis[0])
    add_tile(mark_halves[1:], mark_others[1:])
    near_tiles = [tiles[0][:, :half_marks], tiles[0][:, half_marks:]]
    far_tiles = tiles[1:]
    stats = jnp.concatenate(tile_stats, 1)
    near, far, across = (lax.ppermute(stats, "dp", swap) for swap in (SWAP_NEAR, SWAP_FAR, ACROSS))
    stats = ordered(lambda *four: (four[0] + four[1]) + (four[2] + four[3]), stats, near, far, across)
    far_basis[1] = arrived(far_basis[1])
    stats = after(stats, far_basis[1])
    stats = stats + over_y(jnp.concatenate([stats[:, marks:], stats[:, :marks]], 1))
    peaks = jnp.sqrt(stats[1:]).reshape(4, half_marks, 1)
    weighed = weigh_call(stats, basis, *far_basis)
    weighed = weighed + over_cores(weighed)
    means = weighed[:1] / total_rows
    scales = 2.0**14 / (1.02 * jnp.maximum(weighed[1:], 1e-30))

    def project(far_rows, near_part):
        return (
            near_part
            + product(far_tiles[0], far_rows[:half_marks])
            + product(far_tiles[1], far_rows[half_marks:])
        )

    def centre(other, part, columns):
        rows = data.shape[0]
        projected = part + jnp.concatenate([other[rows:], other[:rows]], 0)
        return (projected - means[:, columns]).astype(jnp.bfloat16), scales[:, columns]

    def part_of(tile, peak, pair):
        centred, scale = pair
        part = lax.dot_general(
            tile, centred, (((0,), (0,)), ((), ())), preferred_element_type=jnp.float32
        )
        return part * (scale * (1.0 / peak))

    def send_step(tile, index, pair):
        return as_half(part_of(tile, peaks[2 + index], pair))

    def panel_step(received, index, pair):
        return as_half(part_of(near_tiles[index], peaks[index], pair) + received.astype(jnp.float32))

    def sum_step(received, kept):
        return as_half(kept.astype(jnp.float32) + received.astype(jnp.float32))

    def final_step(given, total, index):
        chosen = jnp.where(inner, total, given).astype(jnp.float32)
        return chosen * (peaks[index] * 2.0**-14)

    def split_step(part):
        middle = part.shape[0] // 2
        top, bottom = part[:middle], part[middle:]
        return jnp.where(second, bottom, top), jnp.where(second, top, bottom)

    def add_step(received, kept):
        return received + kept

    def gather_step(others, kept):
        return jnp.concatenate(
            [jnp.where(second, others, kept), jnp.where(second, kept, others)], 0
        )

    spans = [slice(0, width), slice(width, 2 * width)]
    first_part = project(far_basis[0], near_parts[0])
    last_part = project(far_basis[1], near_parts[1])
    last_other = over_cores(after(last_part, means))
    centred = [ordered(centre, over_cores(first_part), first_part, spans[0])]
    chunks = [(0, centred[0]), (1, centred[0])]
    received = [None] * 4

    def send(i):
        index, pair = chunks[i]
        received[i] = over_y(ordered(send_step, far_tiles[index], index, pair))

    panels, outers, pairs, crosses, totals, givens, finals = ([None] * 4 for _ in range(7))

    def panel(i):
        panels[i] = ordered(panel_step, received[i], *chunks[i])
        outers[i] = lax.ppermute(panels[i], "dp", TO_INNER)

    def joint(i):
        pairs[i] = ordered(sum_step, outers[i], panels[i])
        crosses[i] = lax.ppermute(pairs[i], "dp", SWAP_INNER)

    def total(i):
        totals[i] = ordered(sum_step, crosses[i], pairs[i])
        givens[i] = lax.ppermute(totals[i], "dp", TO_OUTER)

    def final(i):
        finals[i] = ordered(final_step, givens[i], totals[i], chunks[i][0])

    send(0)
    send(1)
    centred.append(ordered(centre, last_other, last_part, spans[1]))
    chunks += [(0, centred[1]), (1, centred[1])]
    panel(0)
    send(2)
    panel(1)
    send(3)
    joint(0)
    panel(2)
    joint(1)
    total(0)
    panel(3)
    joint(2)
    total(1)
    joint(3)
    total(2)
    final(0)
    final(1)
    first = jnp.concatenate(finals[:2], 0)
    kept, sent = split_step(ordered(gram_call, *finals[:2]))
    arriving = over_cores(sent)
    total(3)
    kept = ordered(add_step, arriving, kept)
    arriving = over_y(kept)
    final(2)
    kept = ordered(add_step, arriving, kept)
    arriving = over_cores(kept)
    final(3)
    last = jnp.concatenate(finals[2:], 0)
    last_kept, last_sent = split_step(product_of(last, jnp.concatenate([first, last], 1)))
    last_kept = last_kept + over_cores(last_sent)
    last_arriving = over_y(last_kept)
    first_gram = gather_step(after(arriving, last_kept), kept)
    done, solve = whiten_first(first_gram, first)
    last_arriving = after(last_arriving, done)
    last_kept = last_kept + last_arriving
    last_gram = gather_step(over_cores(last_kept), last_kept)
    return whiten_second(last_gram, last, done, solve, math.sqrt(all_marks))


def solution(mesh):
    in_specs = (
        P(("groups", "blk", "dp"), None),
        P(("groups", "blk"), None),
        P(("groups", "blk"), None),
    )
    out_specs = P(("groups", "blk"), None)
    fits = mesh.shape["blk"] == 4 and mesh.shape["dp"] == 4
    return jax.shard_map(
        body if fits else general_body,
        mesh=mesh,
        in_specs=in_specs,
        out_specs=out_specs,
        check_vma=False,
    )
```

```python
import functools
import math

import jax
import jax.numpy as jnp
from jax import lax
from jax.experimental import pallas as pl
from jax.experimental.pallas import tpu as pltpu
from jax.sharding import PartitionSpec as P

NORM_EPS = 1e-06
BLOCK = 128
PANEL = 8
HIGHEST = lax.Precision.HIGHEST
SWAP_CORE = [(0, 1), (1, 0), (2, 3), (3, 2)]
SWAP_Y = [(0, 2), (2, 0), (1, 3), (3, 1)]
SWAP_INNER = [(1, 2), (2, 1)]
TO_INNER = [(0, 1), (3, 2)]
TO_OUTER = [(1, 0), (2, 3)]
SWAP_NEAR = [(0, 1), (1, 0), (2, 3), (3, 2)]
ACROSS = [(0, 3), (3, 0), (1, 2), (2, 1)]
SWAP_FAR = [(0, 2), (2, 0), (1, 3), (3, 1)]


def unit_rows(values):
    wide = values.astype(jnp.float32)
    return (wide * lax.rsqrt(jnp.sum(wide * wide, axis=1, keepdims=True) + NORM_EPS)).astype(
        jnp.bfloat16
    )


def kernel_tile(unit_data, unit_marks, exponent_scale):
    scores = lax.dot_general(
        unit_data, unit_marks, (((1,), (1,)), ((), ())), preferred_element_type=jnp.float32
    )
    return jnp.exp(exponent_scale * scores).astype(jnp.bfloat16)


def spread_row(tile, row):
    return jnp.broadcast_to(tile[row : row + 1, :], tile.shape)


def eliminate_panel(square_ref, inverse_ref, panel, low, high):
    size = square_ref.shape[0]
    lane = lax.broadcasted_iota(jnp.int32, (PANEL, size), 1)
    sublane = lax.broadcasted_iota(jnp.int32, (PANEL, size), 0)
    here = pl.ds(pl.multiple_of(panel * PANEL, PANEL), PANEL)

    def columns_of(rows):
        return [jnp.broadcast_to(rows[:, k : k + 1], (PANEL, size)) for k in range(PANEL)]

    head = square_ref[here, :]
    head_columns = columns_of(head)
    scaled, ratios, finished = [], [], jnp.zeros_like(head)
    for k in range(PANEL):
        pivot = spread_row(head_columns[k], k)
        inverse = 1.0 / pivot
        row = jnp.where(lane == k, 1.0, spread_row(head, k))
        finished = jnp.where(sublane == k, row * lax.rsqrt(pivot), finished)
        scaled.append(row * inverse)
        ratios.append({m: spread_row(head_columns[k], m) * inverse for m in range(k + 1, PANEL)})
        for m in range(k + 1, PANEL):
            head_columns[m] = head_columns[m] - head_columns[k] * ratios[k][m]
        head = jnp.where(lane == k, 0.0, head) - head_columns[k] * scaled[k]
    finished = pltpu.roll(finished, panel * PANEL, 1)
    inverse_ref[here, :] = jnp.where(lane <= panel * PANEL + sublane, finished, 0.0)
    weights = [jnp.where((lane <= k) | (lane >= PANEL), scaled[k], 0.0) for k in range(PANEL)]
    for k in reversed(range(PANEL)):
        for m in range(k + 1, PANEL):
            weights[k] = weights[k] - ratios[k][m] * weights[m]
    for g in range(low, high):
        rows = square_ref[PANEL * g : PANEL * (g + 1), :]
        columns = columns_of(rows)
        rows = jnp.where(lane < PANEL, 0.0, rows)
        for k in range(PANEL):
            rows = rows - columns[k] * weights[k]
        square_ref[PANEL * g : PANEL * (g + 1), :] = pltpu.roll(rows, size - PANEL, 1)


def lower_inverse(square_ref, inverse_ref):
    groups = square_ref.shape[0] // PANEL
    spans = 8

    for low in range(0, groups, groups // spans):

        def step(panel, carry):
            eliminate_panel(square_ref, inverse_ref, panel, low, groups)
            return carry

        lax.fori_loop(low, low + groups // spans, step, 0)


def times_transposed(left, right):
    return lax.dot_general(
        left,
        right,
        (((1,), (1,)), ((), ())),
        precision=HIGHEST,
        preferred_element_type=jnp.float32,
    )


def eliminate(scale, left_ref, rows_ref, inverse_ref, square_ref, write):
    order = left_ref.shape[0]
    blocks = order // BLOCK

    def step(position, carry):
        here = pl.ds(pl.multiple_of(position * BLOCK, BLOCK), BLOCK)
        square_ref[...] = left_ref[here, here]
        lower_inverse(square_ref, inverse_ref)
        for b in range(blocks):

            @pl.when(position == b)
            def _():
                now = slice(b * BLOCK, (b + 1) * BLOCK)
                later = slice((b + 1) * BLOCK, order)
                inverse = inverse_ref[...]
                solved = times_transposed(rows_ref[:, now], inverse)
                if b + 1 < blocks:
                    factor = times_transposed(left_ref[later, now], inverse)
                    left_ref[later, later] -= times_transposed(factor, factor)
                    rows_ref[:, later] -= times_transposed(solved, factor)
                write(now, solved * scale)

        return carry

    lax.fori_loop(0, blocks, step, 0)


def whiten_kernel(scale, gram_ref, rows_ref, out_ref, left_ref, moved_ref, inverse_ref, square_ref):
    left_ref[...] = gram_ref[...]
    moved_ref[...] = rows_ref[...]

    def write(now, values):
        out_ref[:, now] = values

    eliminate(scale, left_ref, moved_ref, inverse_ref, square_ref, write)


def first_kernel(gram_ref, rows_ref, out_ref, back_ref, left_ref, moved_ref, inverse_ref, square_ref):
    count, order = rows_ref.shape
    left_ref[...] = gram_ref[...]
    moved_ref[:count, :] = rows_ref[...]
    shape = (order, order)
    moved_ref[count:, :] = jnp.where(
        lax.broadcasted_iota(jnp.int32, shape, 0) == lax.broadcasted_iota(jnp.int32, shape, 1),
        1.0,
        0.0,
    )

    def write(now, values):
        out_ref[:, now] = values[:count]
        back_ref[:, now] = values[count:]

    eliminate(1.0, left_ref, moved_ref, inverse_ref, square_ref, write)


def second_kernel(
    scale, gram_ref, rows_ref, done_ref, solve_ref, out_ref, left_ref, moved_ref, inverse_ref, square_ref
):
    order = rows_ref.shape[1]
    factor = lax.dot_general(
        gram_ref[:, :order],
        solve_ref[...],
        (((1,), (0,)), ((), ())),
        precision=HIGHEST,
        preferred_element_type=jnp.float32,
    )
    left_ref[...] = gram_ref[:, order:] - times_transposed(factor, factor)
    moved_ref[...] = rows_ref[...] - times_transposed(done_ref[...], factor)
    out_ref[:, :order] = done_ref[...] * scale

    def write(now, values):
        out_ref[:, order + now.start : order + now.stop] = values

    eliminate(scale, left_ref, moved_ref, inverse_ref, square_ref, write)


def solve_call(kernel, out_shapes, moved_shape, *operands):
    vmem = pl.BlockSpec(memory_space=pltpu.VMEM)
    single = len(out_shapes) == 1
    shapes = [jax.ShapeDtypeStruct(shape, jnp.float32) for shape in out_shapes]
    order = moved_shape[1]
    return pl.pallas_call(
        kernel,
        out_shape=shapes[0] if single else shapes,
        in_specs=[vmem] * len(operands),
        out_specs=vmem if single else [vmem] * len(shapes),
        scratch_shapes=[
            pltpu.VMEM((order, order), jnp.float32),
            pltpu.VMEM(moved_shape, jnp.float32),
            pltpu.VMEM((BLOCK, BLOCK), jnp.float32),
            pltpu.VMEM((BLOCK, BLOCK), jnp.float32),
        ],
        compiler_params=pltpu.CompilerParams(vmem_limit_bytes=32 * 2**20),
        cost_estimate=pl.CostEstimate(
            flops=160 * moved_shape[0] * order * order,
            bytes_accessed=4 * moved_shape[0] * order,
            transcendentals=0,
        ),
    )(*operands)


def whiten(gram_matrix, rows, scale):
    kernel = functools.partial(whiten_kernel, scale)
    return solve_call(kernel, [rows.shape], rows.shape, gram_matrix, rows)


def whiten_first(gram_matrix, rows):
    count, order = rows.shape
    return solve_call(
        first_kernel, [rows.shape, (order, order)], (count + order, order), gram_matrix, rows
    )


def whiten_second(gram_rows, rows, done, solve, scale):
    count, order = rows.shape
    kernel = functools.partial(second_kernel, scale)
    return solve_call(
        kernel, [(count, 2 * order)], rows.shape, gram_rows, rows, done, solve
    )


def own_gram(rows):
    return lax.dot_general(rows, rows, (((0,), (0,)), ((), ())), precision=HIGHEST)


def general_body(data, landmarks, basis):
    exponent_scale = math.sqrt(data.shape[1])
    all_marks = landmarks.shape[0] * lax.axis_size("blk")
    total_rows = data.shape[0] * lax.axis_size("blk") * lax.axis_size("dp")
    tile = kernel_tile(
        unit_rows(data),
        lax.all_gather(unit_rows(landmarks), "blk", axis=0, tiled=True),
        exponent_scale,
    )
    projected = jnp.dot(
        tile, lax.all_gather(basis, "blk", axis=0, tiled=True), preferred_element_type=jnp.float32
    )
    column_sums = lax.psum(lax.psum(jnp.sum(projected, axis=0), "blk"), "dp")
    centred = (projected - column_sums / total_rows).astype(jnp.bfloat16)
    partial = lax.dot_general(
        tile, centred, (((0,), (0,)), ((), ())), preferred_element_type=jnp.float32
    )
    panel = lax.psum_scatter(partial, "blk", scatter_dimension=0, tiled=True)
    shares = lax.psum_scatter(panel, "dp", scatter_dimension=0, tiled=True)
    gram_matrix = lax.psum(own_gram(shares), ("blk", "dp"))
    local_rows = whiten(gram_matrix, shares, math.sqrt(all_marks))
    return lax.all_gather(local_rows, "dp", axis=0, tiled=True)


def tile_kernel(exponent_scale, split, data_ref, odd_ref, *refs):
    half_refs, other_refs = refs[:split], refs[split:-3]
    tile_ref, stats_ref, unit_ref = refs[-3:]
    at = 0
    if other_refs:
        odd = odd_ref[0] == 1
        for half_ref, other_ref in zip(half_refs, other_refs):
            count, width = half_ref.shape
            here = slice(at, at + count)
            for low in (True, False):
                span = slice(0, width) if low else slice(width, 2 * width)

                @pl.when(odd == low)
                def _():
                    unit_ref[here, span] = other_ref[...]

                @pl.when(odd != low)
                def _():
                    unit_ref[here, span] = half_ref[...]

            at += count
        unit_ref[...] = unit_rows(unit_ref[...])
    else:
        unit_ref[...] = unit_rows(half_refs[0][...])
    rows = data_ref.shape[0]
    step = math.gcd(rows, 480)

    def add_rows(index, stats):
        here = pl.ds(pl.multiple_of(index * step, step), step)
        scores = lax.dot_general(
            data_ref[here, :],
            unit_ref[...],
            (((1,), (1,)), ((), ())),
            preferred_element_type=jnp.float32,
        )
        tile = jnp.exp2(exponent_scale * math.log2(math.e) * scores).astype(jnp.bfloat16)
        tile_ref[here, :] = tile
        wide = tile.astype(jnp.float32)
        return stats[0] + jnp.sum(wide, axis=0, keepdims=True), stats[1] + jnp.sum(
            wide * wide, axis=0, keepdims=True
        )

    none = jnp.zeros((1, unit_ref.shape[0]), jnp.float32)
    stats_ref[...] = jnp.concatenate(lax.fori_loop(0, rows // step, add_rows, (none, none), unroll=2), 0)


def tile_call(unit_data, odd, halves, others, exponent_scale):
    vmem = pl.BlockSpec(memory_space=pltpu.VMEM)
    rows, depth = unit_data.shape
    count = sum(half.shape[0] for half in halves)
    return pl.pallas_call(
        functools.partial(tile_kernel, exponent_scale, len(halves)),
        out_shape=[
            jax.ShapeDtypeStruct((rows, count), jnp.bfloat16),
            jax.ShapeDtypeStruct((2, count), jnp.float32),
        ],
        in_specs=[vmem, pl.BlockSpec(memory_space=pltpu.SMEM)] + [vmem] * (len(halves) + len(others)),
        out_specs=[vmem, vmem],
        scratch_shapes=[pltpu.VMEM((count, depth), jnp.bfloat16)],
        compiler_params=pltpu.CompilerParams(vmem_limit_bytes=32 * 2**20),
        cost_estimate=pl.CostEstimate(
            flops=2 * rows * count * depth,
            bytes_accessed=2 * rows * (count + depth),
            transcendentals=rows * count,
        ),
    )(unit_data, odd, *halves, *others)


def over_cores(values):
    return lax.ppermute(values, "blk", SWAP_CORE)


def over_y(values):
    return lax.ppermute(values, "blk", SWAP_Y)


def after(values, *others):
    return lax.optimization_barrier((values, *others))[0]


def product_of(left, right):
    return lax.dot_general(left, right, (((0,), (0,)), ((), ())), precision=HIGHEST)


def product(left, right):
    return jnp.dot(left, right, preferred_element_type=jnp.float32)


def weigh_kernel(stats_ref, near_ref, first_ref, last_ref, out_ref):
    count, width = first_ref.shape

    def split(weights):
        top = weights.astype(jnp.bfloat16).astype(jnp.float32)
        middle = (weights - top).astype(jnp.bfloat16).astype(jnp.float32)
        low = weights - top - middle
        row = lax.broadcasted_iota(jnp.int32, (8, count), 0)
        parts = jnp.where(row == 0, top, jnp.where(row == 1, middle, jnp.where(row == 2, low, 0.0)))
        return parts.astype(jnp.bfloat16)

    near, far = split(stats_ref[:1, :count]), split(stats_ref[:1, count:])
    for index, far_ref in enumerate((first_ref, last_ref)):
        span = slice(index * width, (index + 1) * width)
        near_rows, far_rows = near_ref[:, span], far_ref[...]
        value = jnp.sum(product(near, near_rows), axis=0, keepdims=True) + jnp.sum(
            product(far, far_rows), axis=0, keepdims=True
        )
        size = product(near, jnp.abs(near_rows)) + product(far, jnp.abs(far_rows))
        out_ref[:, span] = jnp.concatenate([value, size[:1]], 0)


def weigh_call(stats, near_rows, first_rows, last_rows):
    return pl.pallas_call(
        weigh_kernel,
        out_shape=jax.ShapeDtypeStruct((2, near_rows.shape[1]), jnp.float32),
        in_specs=[pl.BlockSpec(memory_space=pltpu.VMEM)] * 4,
        out_specs=pl.BlockSpec(memory_space=pltpu.VMEM),
        compiler_params=pltpu.CompilerParams(vmem_limit_bytes=16 * 2**20),
    )(stats, near_rows, first_rows, last_rows)


def gram_kernel(upper_ref, lower_ref, out_ref):
    upper, lower = upper_ref[...], lower_ref[...]
    out_ref[...] = product_of(upper, upper) + product_of(lower, lower)


def gram_call(upper, lower):
    rows, order = upper.shape
    vmem = pl.BlockSpec(memory_space=pltpu.VMEM)
    return pl.pallas_call(
        gram_kernel,
        out_shape=jax.ShapeDtypeStruct((order, order), jnp.float32),
        in_specs=[vmem, vmem],
        out_specs=vmem,
        compiler_params=pltpu.CompilerParams(vmem_limit_bytes=16 * 2**20),
        cost_estimate=pl.CostEstimate(
            flops=24 * rows * order * order, bytes_accessed=8 * rows * order, transcendentals=0
        ),
    )(upper, lower)


def as_half(values):
    return lax.optimization_barrier(values.astype(jnp.float16))


def body(data, landmarks, basis):
    exponent_scale = math.sqrt(data.shape[1])
    all_marks = landmarks.shape[0] * lax.axis_size("blk")
    total_rows = data.shape[0] * lax.axis_size("blk") * lax.axis_size("dp")
    second = lax.axis_index("blk") % 2 == 1
    place = lax.axis_index("dp")
    odd = place % 2 == 1
    inner = (place == 1) | (place == 2)
    marks = landmarks.shape[0]
    half_marks = marks // 2
    width = basis.shape[1] // 2

    previous = []

    def ordered(step, operand, *others):
        if previous:
            operand = lax.optimization_barrier((operand, previous.pop()))[0]
        value = step(operand, *others)
        previous.append(jax.tree.leaves(value)[0])
        return value

    def own_half(values):
        middle = values.shape[1] // 2
        return jnp.where(odd, values[:, middle:], values[:, :middle])

    def over_near(values):
        return lax.ppermute(values, "dp", SWAP_NEAR)

    basis_parts = [basis[:, :width], basis[:, width:]]
    near_marks = [landmarks[:half_marks], landmarks[half_marks:]]
    first_half = own_half(near_marks[0])
    received = [over_y(first_half)]
    other_data = over_cores(data)
    second_half = own_half(after(near_marks[1], other_data, first_half))
    received.append(over_y(second_half))
    unit_data = unit_rows(jnp.concatenate([after(data, second_half), other_data], 0))
    parity = (place % 2).astype(jnp.int32).reshape(1)
    tiles, tile_stats = [], []

    def add_tile(halves, others=()):
        tile, stats = ordered(
            lambda first: tile_call(unit_data, parity, [first, *halves[1:]], others, exponent_scale),
            halves[0],
        )
        tiles.append(tile)
        tile_stats.append(stats)

    def arrived(values):
        return ordered(lambda value: value, values)

    def mark_arrived(index):
        mark_halves.append(arrived(received[index]))
        mark_others.append(over_near(mark_halves[index]))

    mark_halves, mark_others = [], []
    add_tile([landmarks])
    far_basis = [over_y(after(basis_parts[0], tiles[0]))]
    mark_arrived(0)
    near_parts = [ordered(product, tiles[0], part) for part in basis_parts]
    far_basis.append(over_y(after(basis_parts[1], *near_parts)))
    mark_arrived(1)
    add_tile(mark_halves[:1], mark_others[:1])
    far_basis[0] = arrived(far_basis[0])
    add_tile(mark_halves[1:], mark_others[1:])
    near_tiles = [tiles[0][:, :half_marks], tiles[0][:, half_marks:]]
    far_tiles = tiles[1:]
    stats = jnp.concatenate(tile_stats, 1)
    near, far, across = (lax.ppermute(stats, "dp", swap) for swap in (SWAP_NEAR, SWAP_FAR, ACROSS))
    stats = ordered(lambda *four: (four[0] + four[1]) + (four[2] + four[3]), stats, near, far, across)
    far_basis[1] = arrived(far_basis[1])
    stats = after(stats, far_basis[1])
    stats = stats + over_y(jnp.concatenate([stats[:, marks:], stats[:, :marks]], 1))
    peaks = jnp.sqrt(stats[1:]).reshape(4, half_marks, 1)
    weighed = weigh_call(stats, basis, *far_basis)
    weighed = weighed + over_cores(weighed)
    means = weighed[:1] / total_rows
    scales = 2.0**14 / (1.02 * jnp.maximum(weighed[1:], 1e-30))

    def project(far_rows, near_part):
        return (
            near_part
            + product(far_tiles[0], far_rows[:half_marks])
            + product(far_tiles[1], far_rows[half_marks:])
        )

    def centre(other, part, columns):
        rows = data.shape[0]
        projected = part + jnp.concatenate([other[rows:], other[:rows]], 0)
        return (projected - means[:, columns]).astype(jnp.bfloat16), scales[:, columns]

    def part_of(tile, peak, pair):
        centred, scale = pair
        part = lax.dot_general(
            tile, centred, (((0,), (0,)), ((), ())), preferred_element_type=jnp.float32
        )
        return part * (scale * (1.0 / peak))

    def send_step(tile, index, pair):
        return as_half(part_of(tile, peaks[2 + index], pair))

    def panel_step(received, index, pair):
        return as_half(part_of(near_tiles[index], peaks[index], pair) + received.astype(jnp.float32))

    def sum_step(received, kept):
        return as_half(kept.astype(jnp.float32) + received.astype(jnp.float32))

    def final_step(given, total, index):
        chosen = jnp.where(inner, total, given).astype(jnp.float32)
        return chosen * (peaks[index] * 2.0**-14)

    def split_step(part):
        middle = part.shape[0] // 2
        top, bottom = part[:middle], part[middle:]
        return jnp.where(second, bottom, top), jnp.where(second, top, bottom)

    def add_step(received, kept):
        return received + kept

    def gather_step(others, kept):
        return jnp.concatenate(
            [jnp.where(second, others, kept), jnp.where(second, kept, others)], 0
        )

    spans = [slice(0, width), slice(width, 2 * width)]
    first_part = project(far_basis[0], near_parts[0])
    last_part = project(far_basis[1], near_parts[1])
    last_other = over_cores(after(last_part, means))
    centred = [ordered(centre, over_cores(first_part), first_part, spans[0])]
    chunks = [(0, centred[0]), (1, centred[0])]
    received = [None] * 4

    def send(i):
        index, pair = chunks[i]
        received[i] = over_y(ordered(send_step, far_tiles[index], index, pair))

    panels, outers, pairs, crosses, totals, givens, finals = ([None] * 4 for _ in range(7))

    def panel(i):
        panels[i] = ordered(panel_step, received[i], *chunks[i])
        outers[i] = lax.ppermute(panels[i], "dp", TO_INNER)

    def joint(i):
        pairs[i] = ordered(sum_step, outers[i], panels[i])
        crosses[i] = lax.ppermute(pairs[i], "dp", SWAP_INNER)

    def total(i):
        totals[i] = ordered(sum_step, crosses[i], pairs[i])
        givens[i] = lax.ppermute(totals[i], "dp", TO_OUTER)

    def final(i):
        finals[i] = ordered(final_step, givens[i], totals[i], chunks[i][0])

    send(0)
    send(1)
    centred.append(ordered(centre, last_other, last_part, spans[1]))
    chunks += [(0, centred[1]), (1, centred[1])]
    panel(0)
    send(2)
    panel(1)
    send(3)
    joint(0)
    panel(2)
    joint(1)
    total(0)
    panel(3)
    joint(2)
    total(1)
    joint(3)
    total(2)
    final(0)
    final(1)
    first = jnp.concatenate(finals[:2], 0)
    kept, sent = split_step(ordered(gram_call, *finals[:2]))
    arriving = over_cores(sent)
    total(3)
    kept = ordered(add_step, arriving, kept)
    arriving = over_y(kept)
    final(2)
    kept = ordered(add_step, arriving, kept)
    arriving = over_cores(kept)
    final(3)
    last = jnp.concatenate(finals[2:], 0)
    last_kept, last_sent = split_step(product_of(last, jnp.concatenate([first, last], 1)))
    last_kept = last_kept + over_cores(last_sent)
    last_arriving = over_y(last_kept)
    first_gram = gather_step(after(arriving, last_kept), kept)
    done, solve = whiten_first(first_gram, first)
    last_arriving = after(last_arriving, done)
    last_kept = last_kept + last_arriving
    last_gram = gather_step(over_cores(last_kept), last_kept)
    return whiten_second(last_gram, last, done, solve, math.sqrt(all_marks))


def solution(mesh):
    in_specs = (
        P(("groups", "blk", "dp"), None),
        P(("groups", "blk"), None),
        P(("groups", "blk"), None),
    )
    out_specs = P(("groups", "blk"), None)
    fits = mesh.shape["blk"] == 4 and mesh.shape["dp"] == 4
    return jax.shard_map(
        body if fits else general_body,
        mesh=mesh,
        in_specs=in_specs,
        out_specs=out_specs,
        check_vma=False,
    )
```
